128 devices in a mesh: shard: 8 (over x_lo, y), replica: 16 (over z, x_hi, core).
Axes of the slice: x: 4 (x_hi: 2, x_lo: 2; x = x_hi * 2 + x_lo), y: 4, z: 4, core: 2. Of those that a mesh axis runs over, the one named last changes fastest.
Arguments:
- tokens: bfloat16 [16, 2048, 1024], P('replica', 'shard'), may hold values from -6 to 6
- norm_in: bfloat16 [1024], P('shard'), may hold values from 0.5 to 1.5
- w_in: bfloat16 [1024, 3072], P('shard'), may hold values from -0.1875 to 0.1875
- conv_w: bfloat16 [1024, 3], P('shard'), may hold values from -3 to 3
- w_out: bfloat16 [1024, 1024], P('shard'), may hold values from -0.1875 to 0.1875
- norm_mid: bfloat16 [1024], P('shard'), may hold values from 0.5 to 1.5
- w_gate: bfloat16 [1024, 4608], P('shard'), may hold values from -0.1875 to 0.1875
- w_up: bfloat16 [1024, 4608], P('shard'), may hold values from -0.1875 to 0.1875
- w_down: bfloat16 [1024, 4608], P('shard'), may hold values from -0.09375 to 0.09375
- cotangent: bfloat16 [16, 2048, 1024], P('replica', 'shard'), may hold values from -6 to 6
Outputs:
- result: bfloat16 [16, 2048, 1024], P('replica', 'shard')
- grad_tokens: float32 [16, 2048, 1024], P('replica', 'shard')
- grad_norm_in: float32 [1024], P('shard')
- grad_w_in: float32 [1024, 3072], P('shard')
- grad_conv_w: float32 [1024, 3], P('shard')
- grad_w_out: float32 [1024, 1024], P('shard')
- grad_norm_mid: float32 [1024], P('shard')
- grad_w_gate: float32 [1024, 4608], P('shard')
- grad_w_up: float32 [1024, 4608], P('shard')
- grad_w_down: float32 [1024, 4608], P('shard')
The draws below stay inside these ranges and needn't reach their ends.
All inputs are finite; a program needn't handle non-finite values.
Results may differ from the reference program's by a relative error of at most 0.011.
Values may be sent and summed in bfloat16 or wider, within the bound.
A program may use at most 256 MiB of HBM per device.

```python
import jax
import jax.numpy as jnp
from jax import lax

D = 1024
FF = 4608
SEQ_LEN = 2048
SEQS = 16


def shard_levels(stream_key, extent, pieces, smallest, high):
    def one(axis_at, shards_of):
        steps = jax.random.uniform(jax.random.fold_in(jax.random.fold_in(stream_key, 6), axis_at), (shards_of,), jnp.float32, smallest / len(pieces), high / len(pieces))
        return jnp.repeat(jnp.exp(steps), extent[axis_at] // shards_of).reshape((-1,) + (1,) * (len(extent) - axis_at - 1))

    factor_of = one(*pieces[0])
    for cut in pieces[1:]:
        factor_of = factor_of * one(*cut)
    return factor_of


def centred(key, extent, deviation, bound, split=(), dtype=jnp.bfloat16):
    loudness = shard_levels(key, extent, split, -0.22, 0.18) if split else 1.0
    entries = jax.random.normal(key, extent, jnp.float32) * deviation * loudness
    return jnp.minimum(jnp.maximum(entries, -bound), bound).astype(dtype)


def setup_inputs(seed: int = 0) -> dict:
    key_of = jax.random.split(jax.random.key(seed), 11)
    tokens = centred(key_of[0], (SEQS, SEQ_LEN, D), 1.0, 6.0, ((0, 16), (1, 8)))
    norm_in = jnp.clip(1.0 + 0.1 * jax.random.normal(key_of[1], (D,), jnp.float32), 0.5, 1.5).astype(jnp.bfloat16)
    w_in = centred(key_of[2], (D, 3 * D), D ** -0.5, 0.1875, ((0, 8),))
    conv_w = centred(key_of[3], (D, 3), 0.5, 3.0, ((0, 8),))
    w_out = centred(key_of[4], (D, D), D ** -0.5, 0.1875, ((0, 8),))
    norm_mid = jnp.clip(1.0 + 0.1 * jax.random.normal(key_of[5], (D,), jnp.float32), 0.5, 1.5).astype(jnp.bfloat16)
    w_gate = centred(key_of[6], (D, FF), D ** -0.5, 0.1875, ((0, 8),))
    w_up = centred(key_of[7], (D, FF), D ** -0.5, 0.1875, ((0, 8),))
    w_down = centred(key_of[8], (D, FF), FF ** -0.5, 0.09375, ((0, 8),))
    cotangent = centred(key_of[9], (SEQS, SEQ_LEN, D), 1.0, 6.0, ((0, 16), (1, 8)))
    return dict(tokens=tokens, norm_in=norm_in, w_in=w_in, conv_w=conv_w, w_out=w_out, norm_mid=norm_mid, w_gate=w_gate, w_up=w_up, w_down=w_down, cotangent=cotangent)


@jax.custom_vjp
def low(v):
    return lax.optimization_barrier(v.astype(jnp.bfloat16)).astype(jnp.float32)

@jax.custom_vjp
def low_back(v):
    return v

def low_keep(v):
    return (low(v), None)

def low_pass(kept, grad):
    return (grad,)

def back_keep(v):
    return (v, None)

def back_low(kept, grad):
    return (low(grad),)
low.defvjp(low_keep, low_pass)
low_back.defvjp(back_keep, back_low)
EPS = 1e-05

def product(left, right):
    return jnp.dot(left, right, precision=lax.Precision.HIGHEST, preferred_element_type=jnp.float32)

def normalize(values):
    return values * lax.rsqrt(lax.optimization_barrier(jnp.mean(values * values, axis=-1, keepdims=True)) + EPS)

def block(tokens, norm_in, w_in, conv_w, w_out, norm_mid, w_gate, w_up, w_down):
    width = tokens.shape[1]
    length = tokens.shape[0]
    act_in = low(normalize(tokens) * norm_in)
    proj = low_back(product(act_in, w_in))
    b_part = proj[:, :width]
    c_part = proj[:, width:2 * width]
    x_part = proj[:, 2 * width:]
    mixed_in = low(b_part * x_part)
    padded = jnp.concatenate([jnp.zeros_like(mixed_in[:2]), mixed_in], axis=0)
    conv_out = conv_w[:, 0] * padded[0:length] + conv_w[:, 1] * padded[1:length + 1] + conv_w[:, 2] * padded[2:length + 2]
    gated = low(c_part * conv_out)
    resid_mid = tokens + low_back(product(gated, w_out))
    act_mid = low(normalize(resid_mid) * norm_mid)
    gate = low_back(product(act_mid, w_gate))
    upper = low_back(product(act_mid, w_up))
    hidden = low(jax.nn.silu(gate) * upper)
    ffn_out = low_back(lax.dot_general(hidden, w_down, (((1,), (1,)), ((), ())), precision=lax.Precision.HIGHEST, preferred_element_type=jnp.float32))
    return resid_mid + ffn_out

def reference(tokens, norm_in, w_in, conv_w, w_out, norm_mid, w_gate, w_up, w_down, cotangent):
    weights = tuple((w.astype(jnp.float32) for w in (norm_in, w_in, conv_w, w_out, norm_mid, w_gate, w_up, w_down)))

    def one_sequence(totals, pair):
        sequence, cot = pair
        output, pull = jax.vjp(block, sequence.astype(jnp.float32), *weights)
        grads = pull(cot.astype(jnp.float32))
        totals = tuple((a + g for a, g in zip(totals, grads[1:])))
        return (totals, (output.astype(jnp.bfloat16), grads[0]))
    start = tuple((jnp.zeros(w.shape, jnp.float32) for w in weights))
    totals, (outputs, grad_in) = lax.scan(one_sequence, start, (tokens, cotangent))
    return (outputs, grad_in, totals[0], totals[1], totals[2], totals[3], totals[4], totals[5], totals[6], totals[7])
```

```python
import jax, jax.numpy as jnp
from jax import lax
from jax.sharding import PartitionSpec as P
from jax.experimental import pallas as pl
from jax.experimental.pallas import tpu as pltpu

MESH = pl.DeviceIdType.MESH
BF = jnp.bfloat16
F32 = jnp.float32
EPS = 1e-05


def place():
    s = lax.axis_index("shard")
    r = lax.axis_index("replica")
    xl, y = s // 4, s % 4
    z, xh, c = r // 4, (r // 2) % 2, r % 2
    return xl, xh, y, z, c


def device(x, y, z, c):
    x, y, z = (x + 4) % 4, (y + 4) % 4, (z + 4) % 4
    return ((x % 2) * 4 + y, z * 4 + (x // 2) * 2 + c)


def remote(src, dst, send, recv, to):
    return pltpu.make_async_remote_copy(
        src_ref=src, dst_ref=dst, send_sem=send, recv_sem=recv, device_id=to, device_id_type=MESH
    )


def greet(devices):
    barrier = pltpu.get_barrier_semaphore()
    for to in devices:
        pl.semaphore_signal(barrier, inc=1, device_id=to, device_id_type=MESH)
    pl.semaphore_wait(barrier, len(devices))


def gather_kernel(w_in, w_out, w_gate, w_up, w_down, small, win, wout, wgu, wd, ext,
    vin, vout, vgu, vd, vext, local_sem, send_sem, recv_sem):
    xl, xh, y, z, c = place()
    x = xh * 2 + xl
    own = xl * 4 + y
    half = win.shape[2] // 3
    ff = wgu.shape[3]
    fh = wd.shape[3]
    width = half * 2
    mine = z % 2
    copies = []
    for i in range(3):
        copies.append((w_in.at[:, pl.ds(pl.multiple_of(i * width + c * half, 128), half)], vin.at[:, pl.ds(i * half, half)]))
    copies.append((small, vext))
    copies.append((w_out, vout))
    copies.append((w_gate.at[:, pl.ds(pl.multiple_of(c * ff, 128), ff)], vgu.at[0]))
    copies.append((w_up.at[:, pl.ds(pl.multiple_of(c * ff, 128), ff)], vgu.at[1]))
    copies.append((w_down.at[:, pl.ds(pl.multiple_of(c * ff, 128), fh)], vd.at[0]))
    copies.append((w_down.at[:, pl.ds(pl.multiple_of(c * ff + fh, 128), fh)], vd.at[1]))
    locals_ = [pltpu.make_async_copy(a, b, local_sem.at[i]) for i, (a, b) in enumerate(copies)]
    for cp in locals_:
        cp.start()
    xp, xm = device(x + 1, y, z, c), device(x - 1, y, z, c)
    yp, ym = device(x, y + 1, z, c), device(x, y - 1, z, c)
    zp, zm = device(x, y, z + 1, c), device(x, y, z - 1, c)
    greet([xp, xm, yp, ym, zp, zm])
    for cp in locals_:
        cp.wait()
    stores = [(vin, win.at[own]), (vout, wout.at[own]), (vext, ext.at[own])]
    for g in (0, 1):
        stores += [(vgu.at[g], wgu.at[g, own]), (vd.at[g], wd.at[g, own])]
    stores = [pltpu.make_async_copy(a, b, local_sem.at[i]) for i, (a, b) in enumerate(stores)]
    for cp in stores:
        cp.start()

    parts = [
        (lambda g, u: wgu.at[g, u], True, vgu.at[mine]),
        (lambda g, u: wd.at[g, u], True, vd.at[mine]),
        (lambda g, u: win.at[u], False, vin),
        (lambda g, u: wout.at[u], False, vout),
        (lambda g, u: ext.at[u], False, vext),
    ]
    rows = win.shape[1]
    hr = rows // 2
    count = [0]
    pending = []

    def fresh():
        k = count[0]
        count[0] += 1
        return k

    def send(view, to, k, src=None):
        cp = remote(view if src is None else src, view, send_sem.at[k], recv_sem.at[k], to)
        cp.start()
        pending.append(cp)

    def got(view, k):
        remote(view, view, send_sem.at[k], recv_sem.at[k], yp).wait_recv()

    def cut(view, h):
        return view.at[pl.ds(h * hr, hr)]

    def at_y(dy):
        return xl * 4 + (y + dy + 4) % 4

    def over(dy):
        return (1 - xl) * 4 + (y + dy + 4) % 4

    keys = {}
    for p, (view, by_z, held) in enumerate(parts):
        for name in ["y+", "y-", "f+", "f-"]:
            keys[p, name] = fresh()
        for dy in (0, -1, 1, 2):
            for h in (0, 1):
                keys[p, "x", dy, h] = fresh()
                if by_z:
                    keys[p, "z", 1, dy, h] = fresh()
                    if dy:
                        keys[p, "z", 0, dy, h] = fresh()

    def send_x(p, dy, h):
        src = None if dy else cut(parts[p][2], h)
        send(cut(parts[p][0](mine, at_y(dy)), h), (xp, xm)[h], keys[p, "x", dy, h], src)

    def send_z(p, other, dy, h):
        if parts[p][1]:
            u = over(dy) if other else at_y(dy)
            send(cut(parts[p][0](mine, u), h), (zp, zm)[h], keys[p, "z", other, dy, h])

    for p, (view, by_z, held) in enumerate(parts):
        send(view(mine, own), yp, keys[p, "y+"], held)
        send(view(mine, own), ym, keys[p, "y-"], held)
        for h in (0, 1):
            send_x(p, 0, h)
    def stage_a(p):
        view, by_z, held = parts[p]
        got(view(mine, at_y(-1)), keys[p, "y+"])
        send(cut(view(mine, at_y(-1)), 0), yp, keys[p, "f+"])
        for h in (0, 1):
            send_x(p, -1, h)
            send_z(p, 0, -1, h)
        got(view(mine, at_y(1)), keys[p, "y-"])
        send(cut(view(mine, at_y(1)), 1), ym, keys[p, "f-"])
        for h in (0, 1):
            send_x(p, 1, h)
            send_z(p, 0, 1, h)

    def stage_b(p):
        view, by_z, held = parts[p]
        for h in (0, 1):
            got(cut(view(mine, at_y(2)), h), keys[p, ("f+", "f-")[h]])
            send_x(p, 2, h)
            send_z(p, 0, 2, h)

    def stage_c(p):
        view, by_z, held = parts[p]
        for dy in (0, -1, 1, 2):
            for h in (0, 1):
                got(cut(view(mine, over(dy)), h), keys[p, "x", dy, h])
                send_z(p, 1, dy, h)

    def stage_d(p):
        view, by_z, held = parts[p]
        if by_z:
            for h in (0, 1):
                for dy in (0, -1, 1, 2):
                    if dy:
                        got(cut(view(1 - mine, at_y(dy)), h), keys[p, "z", 0, dy, h])
                    got(cut(view(1 - mine, over(dy)), h), keys[p, "z", 1, dy, h])

    n = len(parts)
    for step in range(n + 3):
        for lag, stage in enumerate((stage_a, stage_b, stage_c, stage_d)):
            if 0 <= step - lag < n:
                stage(step - lag)
    for cp in pending:
        cp.wait_send()
    for cp in stores:
        cp.wait()


COPIES = 5 * 12 + 2 * 14


def gather_weights(w_in, w_out, w_gate, w_up, w_down, small):
    rows = w_in.shape[0]
    groups = 8
    width = w_out.shape[1]
    ff = w_gate.shape[1] // 2
    hbm = pl.BlockSpec(memory_space=pltpu.HBM)
    return pl.pallas_call(
        gather_kernel,
        out_shape=(
            jax.ShapeDtypeStruct((groups, rows, width // 2 * 3), BF),
            jax.ShapeDtypeStruct((groups, rows, width), BF),
            jax.ShapeDtypeStruct((2, groups, rows, ff), BF),
            jax.ShapeDtypeStruct((2, groups, rows, ff // 2), BF),
            jax.ShapeDtypeStruct((groups, rows, 128), BF),
        ),
        in_specs=[hbm] * 6,
        out_specs=(hbm,) * 5,
        scratch_shapes=[
            pltpu.VMEM((rows, width // 2 * 3), BF),
            pltpu.VMEM((rows, width), BF),
            pltpu.VMEM((2, rows, ff), BF),
            pltpu.VMEM((2, rows, ff // 2), BF),
            pltpu.VMEM((rows, 128), BF),
            pltpu.SemaphoreType.DMA((9,)),
            pltpu.SemaphoreType.DMA((COPIES,)),
            pltpu.SemaphoreType.DMA((COPIES,)),
        ],
        compiler_params=pltpu.CompilerParams(collective_id=1, has_side_effects=True),
    )(w_in, w_out, w_gate, w_up, w_down, small)


ORDERS = ("XYZ", "YZX", "ZXY")
SIZES = {"X": (1, 4, 1, 4), "Y": (2, 1, 2, 4), "Z": (2, 4, 2, 1)}


def dims_left(order, phase):
    sizes = [2, 4, 2, 4]
    for axis in order[: phase + 1]:
        for i in {"X": (0, 2), "Y": (1,), "Z": (3,)}[axis]:
            sizes[i] = 1
    return tuple(n for n in sizes if n > 1)


def halves(columns):
    first = columns // 256 * 128
    return (0, first), (first, columns - first)


def reduce_kernel(*refs):
    n = 3
    parts, outs, held = refs[:n], refs[n : 2 * n], refs[2 * n : 3 * n]
    relay = [refs[3 * n + 6 * t : 3 * n + 6 * t + 6] for t in range(n)]
    local_sem, send_sem, recv_sem, spread_send, spread_recv, core_send, core_recv = refs[9 * n :][n * 6 :]
    takes = [refs[9 * n + 6 * t : 9 * n + 6 * t + 6] for t in range(n)]
    xl, xh, y, z, c = place()
    x = xh * 2 + xl
    loads = [pltpu.make_async_copy(parts[t], held[t], local_sem.at[t]) for t in range(n)]
    for cp in loads:
        cp.start()
    where = {"X": x, "Y": y, "Z": z}
    near = {
        "X": (device(x - 1, y, z, c), device(x + 1, y, z, c)),
        "Y": (device(x, y - 1, z, c), device(x, y + 1, z, c)),
        "Z": (device(x, y, z - 1, c), device(x, y, z + 1, c)),
    }
    replicas = [(dx, dz) for dx in (0, 2) for dz in (1, 3, 2, 0) if dx or dz]
    spread_to = [device(x + dx, y, z + dz, c) for dx, dz in replicas]
    sibling = device(x, y, z, 1 - c)
    far = [device(x + dx, y, z + dz, c) for dx, dz in replicas if (dx, dz) not in ((0, 1), (0, 3))]
    greet([*near["X"], *near["Y"], *near["Z"], *far, sibling])
    pending = []

    def index(order, phase, q):
        at = [slice(None)] * 4
        for a in order[:phase]:
            put(at, a, where[a])
        put(at, order[phase], q)
        return tuple(at)

    def put(at, axis, q):
        if axis == "X":
            at[0], at[2] = q % 2, q // 2
        else:
            at[1 if axis == "Y" else 3] = q

    def key(t, phase, k):
        return (t * 3 + phase) * 6 + k

    def ship(src, dst, to, t, phase, k):
        cp = remote(src, dst, send_sem.at[key(t, phase, k)], recv_sem.at[key(t, phase, k)], to)
        cp.start()
        pending.append(cp)

    def arrived(dst, t, phase, k):
        remote(dst, dst, send_sem.at[key(t, phase, k)], recv_sem.at[key(t, phase, k)], sibling).wait_recv()

    def cols(view, h, t):
        at, size = halves(held[t].shape[-1])[h]
        lead = len(view.shape) - 1
        return view.at[(slice(None),) * lead + (pl.ds(at, size),)]

    def part(ref, t, phase, q, h):
        return cols(ref.at[index(ORDERS[t], phase, q)], h, t)

    def buffers(t, phase):
        ra, rb = relay[t][2 * phase : 2 * phase + 2]
        tl, tr = takes[t][2 * phase : 2 * phase + 2]
        return ra, rb, tl, tr

    def each(dims, body):
        total = 1
        for d in dims:
            total *= d

        def step(i, carry):
            at, rest = [], i
            for d in reversed(dims):
                at.append(rest % d)
                rest = rest // d
            body(tuple(reversed(at)))
            return carry

        if total == 1:
            body(())
        else:
            lax.fori_loop(0, total, step, 0)

    def full(order, phase, q, at):
        idx, k = list(index(order, phase, q)), 0
        for i in range(4):
            if isinstance(idx[i], slice):
                idx[i] = at[k]
                k += 1
        return tuple(idx)

    def begin(t, phase):
        order = ORDERS[t]
        p = where[order[phase]]
        left, right = near[order[phase]]
        ra, rb, tl, tr = buffers(t, phase)
        src = parts[t] if phase == 0 else held[t]
        far_q, next_q, last_q = (p + 2) % 4, (p + 1) % 4, (p + 3) % 4
        ship(part(src, t, phase, far_q, 0), ra, right, t, phase, 0)
        ship(part(src, t, phase, far_q, 1), rb, left, t, phase, 1)
        ship(part(src, t, phase, next_q, 1), cols(tl, 1, t), right, t, phase, 2)
        ship(part(src, t, phase, last_q, 0), cols(tr, 0, t), left, t, phase, 3)

    def middle(t, phase):
        order = ORDERS[t]
        p = where[order[phase]]
        left, right = near[order[phase]]
        ra, rb, tl, tr = buffers(t, phase)
        dims = dims_left(order, phase)
        if phase == 0:
            loads[t].wait()
        for h, (box, q, to, dst) in enumerate(((ra, (p + 1) % 4, right, tl), (rb, (p + 3) % 4, left, tr))):
            arrived(box, t, phase, h)
            at0, size = halves(held[t].shape[-1])[h]

            def add(at, box=box, q=q, at0=at0, size=size):
                slab = full(order, phase, q, at) + (slice(None), pl.ds(at0, size))
                held[t][slab] = (held[t][slab].astype(F32) + box[at].astype(F32)).astype(BF)

            each(dims, add)
            ship(part(held[t], t, phase, q, h), cols(dst, h, t), to, t, phase, 4 + h)

    def finish(t, phase):
        order = ORDERS[t]
        p = where[order[phase]]
        ra, rb, tl, tr = buffers(t, phase)
        dims = dims_left(order, phase)
        arrived(cols(tl, 1, t), t, phase, 2)
        arrived(cols(tr, 0, t), t, phase, 3)
        arrived(cols(tl, 0, t), t, phase, 4)
        arrived(cols(tr, 1, t), t, phase, 5)

        def add(at):
            slab = full(order, phase, p, at)
            held[t][slab] = (held[t][slab].astype(F32) + tl[at].astype(F32) + tr[at].astype(F32)).astype(BF)

        each(dims, add)

    for phase in range(3):
        for t in range(n):
            begin(t, phase)
        for t in range(n):
            middle(t, phase)
        for t in range(n):
            finish(t, phase)
    slot = xh * 4 + z
    for t in range(n):
        piece = held[t].at[xl, y, xh, z]
        for i, to in enumerate(spread_to):
            cp = remote(piece, outs[t].at[c, slot], spread_send.at[t * 7 + i], spread_recv.at[t * 7 + i], to)
            cp.start()
            pending.append(cp)
    keeps = [pltpu.make_async_copy(held[t].at[xl, y, xh, z], outs[t].at[c, slot], local_sem.at[t]) for t in range(n)]
    for cp in keeps:
        cp.start()
    for t in range(n):
        keeps[t].wait()
        for i, (dx, dz) in enumerate(replicas):
            src = ((xh + dx // 2) % 2) * 4 + (z + 4 - dz) % 4
            dst = outs[t].at[c, src]
            remote(dst, dst, spread_send.at[t * 7 + i], spread_recv.at[t * 7 + i], sibling).wait_recv()
        cp = remote(outs[t].at[c], outs[t].at[c], core_send.at[t], core_recv.at[t], sibling)
        cp.start()
        pending.append(cp)
    for t in range(n):
        dst = outs[t].at[1 - c]
        remote(dst, dst, core_send.at[t], core_recv.at[t], sibling).wait_recv()
    for cp in pending:
        cp.wait_send()


def reduce_grads(parts):
    n = len(parts)
    widths = [p.shape[1] for p in parts]
    parts = [p.reshape(2, 4, 2, 4, p.shape[0] // 64, p.shape[1]) for p in parts]
    rows = parts[0].shape[4]
    held = [pltpu.VMEM(p.shape, BF) for p in parts]
    relay, takes = [], []
    for t in range(n):
        for phase in range(3):
            dims = dims_left(ORDERS[t], phase)
            for h in (0, 1):
                relay.append(pltpu.VMEM(dims + (rows, halves(widths[t])[h][1]), BF))
                takes.append(pltpu.VMEM(dims + (rows, widths[t]), BF))
    dma = pltpu.SemaphoreType.DMA
    hbm = pl.BlockSpec(memory_space=pltpu.HBM)
    return pl.pallas_call(
        reduce_kernel,
        out_shape=tuple(jax.ShapeDtypeStruct((2, 8, rows, w), BF) for w in widths),
        in_specs=[hbm] * n,
        out_specs=(hbm,) * n,
        scratch_shapes=held + relay + takes + [dma((3,)), dma((54,)), dma((54,)), dma((21,)), dma((21,)), dma((3,)), dma((3,))],
        compiler_params=pltpu.CompilerParams(collective_id=2, has_side_effects=True, vmem_limit_bytes=56 << 20),
    )(*parts)


def swap(array):
    count = lax.axis_size("replica")
    return lax.ppermute(array, "replica", [(i, i ^ 1) for i in range(count)])


def both(array):
    return jnp.concatenate([array[None], swap(array)[None]], axis=0)


def combine(partial):
    return partial[0] + swap(partial[1])


def shifted(array, axis, by):
    count = lax.axis_size(axis)
    pairs = [(i, i + by) for i in range(count) if 0 <= i + by < count]
    return lax.ppermute(array, axis, pairs)


def normalize(values):
    scale = lax.rsqrt(jnp.mean(values * values, axis=-1, keepdims=True) + EPS)
    return (values * scale, scale)


def norm_back(grad_normed, normed, scale):
    return scale * (grad_normed - normed * jnp.mean(grad_normed * normed, axis=-1, keepdims=True))


def mul(left, right):
    return lax.dot_general(left, right, (((1,), (0,)), ((), ())), preferred_element_type=F32)


def times_rows(left, right):
    return lax.dot_general(left, right, (((1,), (1,)), ((), ())), preferred_element_type=F32)


def cross_rows(left, right):
    return lax.dot_general(left, right, (((0,), (0,)), ((), ())), preferred_element_type=F32).astype(BF)


def local(tokens, norm_in, w_in, conv_w, w_out, norm_mid, w_gate, w_up, w_down, cotangent):
    length, width = tokens.shape[1], tokens.shape[2]
    half = width // 2
    core = lax.axis_index("replica") % 2
    rows = w_in.shape[0]
    small = jnp.concatenate(
        [norm_in[:, None], norm_mid[:, None], conv_w, jnp.zeros((rows, 128 - 5), BF)], axis=1
    )
    win, wout, wgu, wd, ext = gather_weights(w_in, w_out, w_gate, w_up, w_down, small)
    win = win.reshape(width, 3 * half)
    wout = wout.reshape(width, width)
    wg, wu = wgu[0].reshape(width, -1), wgu[1].reshape(width, -1)
    wd0, wd1 = wd[0].reshape(width, -1), wd[1].reshape(width, -1)
    ext = ext.reshape(width, 128)[:, :8].astype(F32).T
    gain_in, gain_mid = ext[0], ext[1]
    taps = lax.dynamic_slice_in_dim(ext[2:5], core * half, half, axis=1)
    wout_mine = lax.dynamic_slice_in_dim(wout, core * half, half, axis=0)

    pair = both(jnp.stack([tokens[0], cotangent[0]]))
    tokens2, cot2 = pair[:, 0].reshape(2 * length, width), pair[:, 1].reshape(2 * length, width)
    normed2, scale2 = normalize(tokens2.astype(F32))
    act_in = (normed2 * gain_in).astype(BF)
    proj = mul(act_in, win)
    b_part, c_part, x_part = (proj[:, i * half : (i + 1) * half].reshape(2, length, half) for i in range(3))
    mixed_in = (b_part * x_part).astype(BF)
    before = shifted(mixed_in[:, length - 2 :], "shard", 1)
    padded = jnp.concatenate([before, mixed_in], axis=1).astype(F32)
    conv_out = sum(taps[k] * padded[:, k : k + length] for k in range(3))
    gated = (c_part * conv_out).astype(BF).reshape(2 * length, half)
    mix = combine(mul(gated, wout_mine).reshape(2, length, width))
    resid_mid = tokens[0].astype(F32) + mix
    normed_mid, scale_mid = normalize(resid_mid)
    act_mid = both((normed_mid * gain_mid).astype(BF)).reshape(2 * length, width)
    gate, up = mul(act_mid, wg), mul(act_mid, wu)
    sig = jax.nn.sigmoid(gate)
    hidden = (gate * sig * up).astype(BF)
    fh = wd0.shape[1]
    ffn = times_rows(hidden[:, :fh], wd0) + times_rows(hidden[:, fh:], wd1)
    result = (resid_mid + combine(ffn.reshape(2, length, width))).astype(BF)
    grad_hidden = jnp.concatenate([mul(cot2, wd0), mul(cot2, wd1)], axis=1)
    grad_gate = (grad_hidden * up * sig * (1.0 + gate * (1.0 - sig))).astype(BF)
    grad_up = (grad_hidden * gate * sig).astype(BF)
    grad_act_mid = combine((times_rows(grad_gate, wg) + times_rows(grad_up, wu)).reshape(2, length, width))
    grad_gain_mid = jnp.sum(grad_act_mid * normed_mid, axis=0)
    grad_resid = cotangent[0].astype(F32) + norm_back(grad_act_mid * gain_mid, normed_mid, scale_mid)
    grad_mix = both(grad_resid.astype(BF)).reshape(2 * length, width)
    grad_gated = times_rows(grad_mix, wout_mine).reshape(2, length, half)
    grad_c = grad_gated * conv_out
    grad_conv = grad_gated * c_part
    grad_taps = jnp.stack([jnp.sum(grad_conv * padded[:, k : k + length], axis=(0, 1)) for k in range(3)])
    after = shifted(grad_conv[:, :2], "shard", -1)
    extended = jnp.concatenate([grad_conv, after], axis=1)
    grad_mixed = sum(taps[2 - k] * extended[:, k : k + length] for k in range(3))
    grad_proj = (
        jnp.concatenate([grad_mixed * x_part, grad_c, grad_mixed * b_part], axis=2)
        .astype(BF)
        .reshape(2 * length, 3 * half)
    )
    grad_act_in = combine(times_rows(grad_proj, win).reshape(2, length, width))
    normed_in, scale_in = normed2[:length], scale2[:length]
    grad_gain_in = jnp.sum(grad_act_in * normed_in, axis=0)
    grad_tokens = grad_resid + norm_back(grad_act_in * gain_in, normed_in, scale_in)

    gains = jnp.stack([grad_gain_in, grad_gain_mid])
    gains = gains + swap(gains)
    spread_taps = lax.dynamic_update_slice_in_dim(
        jnp.zeros((3, width), F32), grad_taps, core * half, axis=1
    )
    spread_taps = spread_taps + swap(spread_taps)
    smalls = jnp.concatenate([gains, spread_taps, jnp.zeros((123, width), F32)], axis=0).T.astype(BF)
    gated_all = swap(gated)
    grad_mix_mine = lax.dynamic_slice_in_dim(grad_mix, core * half, half, axis=1)
    swapped_back = jnp.concatenate([gated_all[length:], gated_all[:length]], axis=0)
    low_half = jnp.where(core == 0, gated, swapped_back)
    high_half = jnp.where(core == 0, swapped_back, gated)
    gated_full = jnp.concatenate([low_half, high_half], axis=1)
    d_in = cross_rows(act_in, grad_proj)
    d_out = cross_rows(gated_full, grad_mix_mine)
    quarter = half // 2
    parts = [
        jnp.concatenate([cross_rows(act_mid, grad_gate), d_in[:, :half], smalls], axis=1),
        jnp.concatenate([cross_rows(act_mid, grad_up), d_in[:, half : 2 * half], d_out[:, :quarter]], axis=1),
        jnp.concatenate([cross_rows(cot2, hidden), d_in[:, 2 * half :], d_out[:, quarter:]], axis=1),
    ]
    ff = hidden.shape[1]
    sums = [s.reshape(2, rows, s.shape[-1]).astype(F32) for s in reduce_grads(parts)]

    def join(pieces):
        return jnp.concatenate(pieces, axis=1)

    g_in = join([sums[i][c, :, ff : ff + half] for i in range(3) for c in (0, 1)])
    g_out = join([sums[i][c, :, ff + half :] for c in (0, 1) for i in (1, 2)])
    g_gate, g_up, g_down = (join([s[0, :, :ff], s[1, :, :ff]]) for s in sums)
    g_small = sums[0][0, :, ff + half :]
    return (
        result[None],
        grad_tokens[None],
        g_small[:, 0],
        g_in,
        g_small[:, 2:5],
        g_out,
        g_small[:, 1],
        g_gate,
        g_up,
        g_down,
    )


def solution(mesh):
    row, act, vec = P("shard", None), P("replica", "shard", None), P("shard")
    in_specs = (act, vec, row, row, row, vec, row, row, row, act)
    out_specs = (act, act, vec, row, row, row, vec, row, row, row)
    return jax.shard_map(local, mesh=mesh, in_specs=in_specs, out_specs=out_specs, check_vma=False)
```

```python
import jax
import jax.numpy as jnp
from jax import lax
from jax.sharding import PartitionSpec as P
from jax.experimental import pallas as pl
from jax.experimental.pallas import tpu as pltpu

MESH = pl.DeviceIdType.MESH
BF = jnp.bfloat16
F32 = jnp.float32
EPS = 1e-05


def place():
    s = lax.axis_index("shard")
    r = lax.axis_index("replica")
    xl, y = s // 4, s % 4
    z, xh, c = r // 4, (r // 2) % 2, r % 2
    return xl, xh, y, z, c


def device(x, y, z, c):
    x, y, z = (x + 4) % 4, (y + 4) % 4, (z + 4) % 4
    return ((x % 2) * 4 + y, z * 4 + (x // 2) * 2 + c)


def remote(src, dst, send, recv, to):
    return pltpu.make_async_remote_copy(
        src_ref=src, dst_ref=dst, send_sem=send, recv_sem=recv, device_id=to, device_id_type=MESH
    )


def greet(devices):
    barrier = pltpu.get_barrier_semaphore()
    for to in devices:
        pl.semaphore_signal(barrier, inc=1, device_id=to, device_id_type=MESH)
    pl.semaphore_wait(barrier, len(devices))


def mul(left, right):
    return lax.dot_general(left, right, (((1,), (0,)), ((), ())), preferred_element_type=F32)


def times_rows(left, right):
    return lax.dot_general(left, right, (((1,), (1,)), ((), ())), preferred_element_type=F32)


def normalize(values):
    scale = lax.rsqrt(jnp.mean(values * values, axis=-1, keepdims=True) + EPS)
    return values * scale, scale


def norm_back(grad_normed, normed, scale):
    return scale * (grad_normed - normed * jnp.mean(grad_normed * normed, axis=-1, keepdims=True))


def loop(count, body):
    def step(i, carry):
        body(i)
        return carry

    lax.fori_loop(0, count, step, 0)


def chunk(i, size):
    return pl.ds(pl.multiple_of(i * size, size), size)


def flat(value):
    return value.reshape(-1, value.shape[-1])


SWAPS = ("tokens", "cot", "gated0", "gated1", "mix", "act", "ffn", "gam", "gmix", "gai", "fore", "back")
TILE = 256


def block_kernel(
    tokens, cot, w_in, w_out, w_gate, w_up, w_down, gains, taps_in,
    result, grad_tokens, o_act_in, o_act_mid, o_hidden, o_gg, o_gu, o_proj, o_gated, o_mix, o_cot, o_small,
    win, wout, wgu, wd, ext, tok2, cot2, act_in, proj, mixed, conv, gated, part, box_mix, box_ffn, box_gam, box_gai,
    resid, normed, act_mid, hidden, fac_a, fac_b, gg, gu, gmix, gconv, gproj, vecs, small, scale_mid, out_res,
    local_sem, send_sem, recv_sem, core_send, core_recv, out_sem,
):
    xl, xh, y, z, c = place()
    x = xh * 2 + xl
    shard, replica = lax.axis_index("shard"), lax.axis_index("replica")
    own = xl * 4 + y
    length, width = tokens.shape
    half = width // 2
    ff = wd.shape[2]
    rows = wd.shape[1]
    mine = z % 2
    xp, xm = device(x + 1, y, z, c), device(x - 1, y, z, c)
    yp, ym = device(x, y + 1, z, c), device(x, y - 1, z, c)
    zp, zm = device(x, y, z + 1, c), device(x, y, z - 1, c)
    sibling = device(x, y, z, 1 - c)
    nxt, prv = ((shard + 1) % 8, replica), ((shard + 7) % 8, replica)
    first, last = shard == 0, shard == 7

    ext[own] = jnp.concatenate([gains[...].astype(F32), taps_in[...].astype(F32), jnp.zeros((27, 128), F32)], axis=0).astype(BF)
    copies = []
    for i in range(3):
        copies.append((w_in.at[:, pl.ds(pl.multiple_of(i * width + c * half, 128), half)], win.at[own, :, pl.ds(i * half, half)]))
    copies.append((w_gate.at[:, pl.ds(pl.multiple_of(c * ff, 128), ff)], wgu.at[0, own]))
    copies.append((w_up.at[:, pl.ds(pl.multiple_of(c * ff, 128), ff)], wgu.at[1, own]))
    copies.append((w_out, wout.at[own]))
    copies.append((w_down.at[:, pl.ds(pl.multiple_of(c * ff, 128), ff)], wd.at[own]))
    copies.append((tokens, tok2.at[pl.ds(0, length)]))
    copies.append((cot, cot2.at[pl.ds(0, length)]))
    loads = [pltpu.make_async_copy(a, b, local_sem.at[i]) for i, (a, b) in enumerate(copies)]
    for cp in loads:
        cp.start()
    greet([xp, xm, yp, ym, zp, zm, sibling, nxt, prv])

    pending = []

    def fire(cp):
        cp.start()
        pending.append(cp.wait_send)

    def swap(name, src, dst, to=None):
        k = SWAPS.index(name)
        return remote(src, dst, core_send.at[k], core_recv.at[k], sibling if to is None else to)

    def wd_part(g, u):
        return wd.at[u, pl.ds(pl.multiple_of(g * (rows // 2), rows // 2), rows // 2)]

    parts = [
        (lambda g, u: ext.at[u], False),
        (lambda g, u: win.at[u], False),
        (lambda g, u: wgu.at[g, u], True),
        (lambda g, u: wout.at[u], False),
        (wd_part, True),
    ]
    keys, count = {}, 0
    for p in range(len(parts)):
        names = ["y+", "y-", "f+", "f-"]
        for dy in (0, -1, 1, 2):
            for h in (0, 1):
                names.append(("x", dy, h))
                if parts[p][1]:
                    names.append(("z", 1, dy, h))
                    if dy:
                        names.append(("z", 0, dy, h))
        for name in names:
            keys[p, name] = count
            count += 1
    assert count == COPIES

    def send(view, to, k):
        fire(remote(view, view, send_sem.at[k], recv_sem.at[k], to))

    def got(view, k):
        remote(view, view, send_sem.at[k], recv_sem.at[k], yp).wait_recv()

    def cut(view, h):
        hr = view.shape[0] // 2
        return view.at[pl.ds(h * hr, hr)]

    def at_y(dy):
        return xl * 4 + (y + dy + 4) % 4

    def over(dy):
        return (1 - xl) * 4 + (y + dy + 4) % 4

    def send_x(p, dy, h):
        send(cut(parts[p][0](mine, at_y(dy)), h), (xp, xm)[h], keys[p, ("x", dy, h)])

    def send_z(p, other, dy, h):
        if parts[p][1]:
            u = over(dy) if other else at_y(dy)
            send(cut(parts[p][0](mine, u), h), (zp, zm)[h], keys[p, ("z", other, dy, h)])

    def launch(p):
        view = parts[p][0]
        send(view(mine, own), yp, keys[p, "y+"])
        send(view(mine, own), ym, keys[p, "y-"])
        for h in (0, 1):
            send_x(p, 0, h)

    def stage_a(p):
        view = parts[p][0]
        got(view(mine, at_y(-1)), keys[p, "y+"])
        send(cut(view(mine, at_y(-1)), 0), yp, keys[p, "f+"])
        for h in (0, 1):
            send_z(p, 0, -1, h)
            send_x(p, -1, h)
        got(view(mine, at_y(1)), keys[p, "y-"])
        send(cut(view(mine, at_y(1)), 1), ym, keys[p, "f-"])
        for h in (0, 1):
            send_z(p, 0, 1, h)
            send_x(p, 1, h)

    def stage_b(p):
        view = parts[p][0]
        for h in (0, 1):
            got(cut(view(mine, at_y(2)), h), keys[p, ("f+", "f-")[h]])
            send_z(p, 0, 2, h)
            send_x(p, 2, h)

    def stage_c(p, dys=(0, -1, 1, 2)):
        view = parts[p][0]
        for dy in dys:
            for h in (0, 1):
                got(cut(view(mine, over(dy)), h), keys[p, ("x", dy, h)])
                send_z(p, 1, dy, h)

    def stage_d(p):
        view = parts[p][0]
        for h in (0, 1):
            for dy in (0, -1, 1, 2):
                if dy:
                    got(cut(view(1 - mine, at_y(dy)), h), keys[p, ("z", 0, dy, h)])
                got(cut(view(1 - mine, over(dy)), h), keys[p, ("z", 1, dy, h)])

    EXT, WIN, WGU, WOUT, WD = range(5)
    lower, upper = pl.ds(0, length), pl.ds(length, length)
    launch(EXT)
    for cp in loads[:3]:
        cp.wait()
    launch(WIN)
    for cp in loads[3:5]:
        cp.wait()
    launch(WGU)
    for cp in loads[7:]:
        cp.wait()
    fire(swap("tokens", tok2.at[lower], tok2.at[upper]))
    fire(swap("cot", cot2.at[lower], cot2.at[upper]))
    for cp in loads[5:7]:
        cp.wait()
    launch(WOUT)
    launch(WD)
    for stage in (stage_a, stage_b, stage_c):
        stage(EXT)
    for u in range(8):
        vecs[:, pl.ds(u * 128, 128)] = ext[u, pl.ds(0, 16)].astype(F32)
    small[...] = jnp.zeros_like(small)
    mixed[:, pl.ds(0, 8)] = jnp.zeros((2, 8, half), F32)
    gconv[:, pl.ds(length, 8)] = jnp.zeros((2, 8, half), F32)
    stage_a(WIN)
    swap("tokens", tok2.at[lower], tok2.at[upper]).wait_recv()
    rc = 32

    def norm_in_step(i):
        v, _ = normalize(tok2[chunk(i, rc)].astype(F32))
        act_in[chunk(i, rc)] = (v * vecs[0:1]).astype(BF)

    loop(2 * length // rc, norm_in_step)
    stage_b(WIN)
    stage_a(WGU)
    stage_c(WIN)

    def proj_step(j):
        proj[:, chunk(j, TILE)] = mul(act_in[...], flat(win[:, :, chunk(j, TILE)]))

    loop(3 * half // TILE, proj_step)

    def b_of(at):
        return proj[at, pl.ds(0, half)]

    def c_of(at):
        return proj[at, pl.ds(half, half)]

    def x_of(at):
        return proj[at, pl.ds(2 * half, half)]

    def mixed_step(i):
        for q in (0, 1):
            at = pl.ds(pl.multiple_of(q * length + i * rc, rc), rc)
            mixed[q, pl.ds(pl.multiple_of(8 + i * rc, 8), rc)] = (b_of(at) * x_of(at)).astype(BF).astype(F32)

    loop(length // rc, mixed_step)
    fore = swap("fore", mixed.at[:, pl.ds(length, 8)], mixed.at[:, pl.ds(0, 8)], nxt)
    back = swap("back", gconv.at[:, pl.ds(0, 8)], gconv.at[:, pl.ds(length, 8)], prv)

    @pl.when(jnp.logical_not(last))
    def _():
        fore.start()

    stage_b(WGU)

    @pl.when(jnp.logical_not(first))
    def _():
        fore.wait_recv()

    taps = [vecs[pl.ds(2 + k, 1), pl.ds(pl.multiple_of(c * half, 128), half)] for k in range(3)]
    rq = 64

    def conv_step(i):
        for q in (0, 1):
            window = mixed[q, pl.ds(pl.multiple_of(i * rq, 8), rq + 8)]
            value = taps[0] * window[6 : 6 + rq] + taps[1] * window[7 : 7 + rq] + taps[2] * window[8 : 8 + rq]
            at = pl.ds(pl.multiple_of(q * length + i * rq, rq), rq)
            conv[at] = value
            gated[at, pl.ds(pl.multiple_of(c * half, 128), half)] = (c_of(at) * value).astype(BF)

    loop(length // rq, conv_step)
    gated_mine = gated.at[:, pl.ds(pl.multiple_of(c * half, 128), half)]
    gated_other = gated.at[:, pl.ds(pl.multiple_of((1 - c) * half, 128), half)]
    fire(swap("gated0", gated_mine.at[lower], gated_mine.at[upper]))
    fire(swap("gated1", gated_mine.at[upper], gated_mine.at[lower]))
    for stage in (stage_a, stage_b, stage_c):
        stage(WOUT)
    wout_mine = wout.at[pl.ds(pl.multiple_of(c * 4, 4), 4)]

    def mix_step(j):
        part[:, chunk(j, TILE)] = mul(gated_mine[...], flat(wout_mine[:, :, chunk(j, TILE)]))

    loop(width // TILE, mix_step)
    mix_swap = swap("mix", part.at[upper], box_mix)
    mix_swap.start()
    stage_c(WGU, (0, -1))
    mix_swap.wait_recv()

    def norm_mid_step(i):
        at = chunk(i, rc)
        v = tok2[at].astype(F32) + part[at] + box_mix[at]
        n, s = normalize(v)
        resid[at] = v
        normed[at] = n
        scale_mid[at] = jnp.broadcast_to(s, (rc, 128))
        act_mid[at] = (n * vecs[1:2]).astype(BF)

    loop(length // rc, norm_mid_step)
    act_swap = swap("act", act_mid.at[lower], act_mid.at[upper])
    act_swap.start()
    stage_c(WGU, (1, 2))
    stage_a(WD)
    act_swap.wait_recv()
    stage_b(WD)
    stage_c(WD)
    stage_d(WGU)

    def gate_step(j):
        at = chunk(j, TILE)
        gate = mul(act_mid[...], flat(wgu[0, :, :, at]))
        up = mul(act_mid[...], flat(wgu[1, :, :, at]))
        sig = jax.nn.sigmoid(gate)
        silu = gate * sig
        hidden[:, at] = (silu * up).astype(BF)
        fac_b[:, at] = silu
        fac_a[:, at] = up * (sig * (1.0 + gate * (1.0 - sig)))

    loop(ff // TILE, gate_step)
    stage_d(WD)
    swap("cot", cot2.at[lower], cot2.at[upper]).wait_recv()

    def grad_hidden_step(j):
        at = chunk(j, TILE)
        g = mul(cot2[...], flat(wd[:, :, at]))
        gg[:, at] = (g * fac_a[:, at]).astype(BF)
        gu[:, at] = (g * fac_b[:, at]).astype(BF)

    loop(ff // TILE, grad_hidden_step)
    swap("mix", part.at[upper], box_mix).wait_send()

    def gam_step(j):
        u = pl.ds(j * 2, 2)
        part[:, chunk(j, TILE)] = times_rows(gg[...], flat(wgu[0, u])) + times_rows(gu[...], flat(wgu[1, u]))

    loop(4, gam_step)
    gam_swap = swap("gam", part.at[upper], box_gam)
    gam_swap.start()
    gam_swap.wait_recv()

    def resid_step(i):
        at = chunk(i, rc)
        g = part[at] + box_gam[at]
        n = normed[at]
        small[1:2] = small[1:2] + jnp.sum(g * n, axis=0, keepdims=True)
        full = cot2[at].astype(F32) + norm_back(g * vecs[1:2], n, scale_mid[at, 0:1])
        box_gam[at] = full
        gmix[at] = full.astype(BF)

    loop(length // rc, resid_step)
    gmix_swap = swap("gmix", gmix.at[lower], gmix.at[upper])
    gmix_swap.start()
    gam_swap.wait_send()

    def ffn_step(j):
        u = pl.ds(j * 2, 2)
        part[:, chunk(j, TILE)] = times_rows(hidden[...], flat(wd[u]))

    loop(4, ffn_step)
    ffn_swap = swap("ffn", part.at[upper], box_ffn)
    ffn_swap.start()
    gmix_swap.wait_recv()
    grad_gated = fac_a.at[:, pl.ds(0, half)]
    grad_gated[...] = times_rows(gmix[...], flat(wout_mine[...]))

    def gconv_step(i):
        for q in (0, 1):
            at = pl.ds(pl.multiple_of(q * length + i * rc, rc), rc)
            window = mixed[q, pl.ds(pl.multiple_of(i * rc, 8), rc + 8)]
            g = grad_gated[at]
            gc = g * c_of(at)
            gconv[q, pl.ds(pl.multiple_of(i * rc, 8), rc)] = gc
            gproj[at, pl.ds(half, half)] = (g * conv[at]).astype(BF)
            for k in range(3):
                spot = (pl.ds(2 + k, 1), pl.ds(pl.multiple_of(c * half, 128), half))
                small[spot] = small[spot] + jnp.sum(gc * window[6 + k : 6 + k + rc], axis=0, keepdims=True)

    loop(length // rc, gconv_step)

    @pl.when(jnp.logical_not(first))
    def _():
        back.start()

    ffn_swap.wait_recv()

    def result_step(i):
        at = chunk(i, rc)
        out_res[at] = (resid[at] + part[at] + box_ffn[at]).astype(BF)

    loop(length // rc, result_step)

    @pl.when(jnp.logical_not(last))
    def _():
        back.wait_recv()

    def gproj_step(i):
        for q in (0, 1):
            at = pl.ds(pl.multiple_of(q * length + i * rc, rc), rc)
            window = gconv[q, pl.ds(pl.multiple_of(i * rc, 8), rc + 8)]
            gm = taps[2] * window[0:rc] + taps[1] * window[1 : rc + 1] + taps[0] * window[2 : rc + 2]
            gproj[at, pl.ds(0, half)] = (gm * x_of(at)).astype(BF)
            gproj[at, pl.ds(2 * half, half)] = (gm * b_of(at)).astype(BF)

    loop(length // rc, gproj_step)
    ffn_swap.wait_send()

    def gai_step(j):
        u = pl.ds(j * 2, 2)
        part[:, chunk(j, TILE)] = times_rows(gproj[...], flat(win[u]))

    loop(4, gai_step)
    gai_swap = swap("gai", part.at[upper], box_gai)
    gai_swap.start()
    swap("gated0", gated_other.at[upper], gated_other.at[upper]).wait_recv()
    swap("gated1", gated_other.at[lower], gated_other.at[lower]).wait_recv()
    stores = [
        (act_in, o_act_in), (act_mid, o_act_mid), (hidden, o_hidden), (gg, o_gg), (gu, o_gu), (gproj, o_proj),
        (gated, o_gated), (gmix, o_mix), (cot2, o_cot), (out_res, result),
    ]
    stores = [pltpu.make_async_copy(a, b, out_sem.at[i]) for i, (a, b) in enumerate(stores)]
    for cp in stores:
        cp.start()
    gai_swap.wait_recv()

    def final_step(i):
        at = chunk(i, rc)
        g = part[at] + box_gai[at]
        n, s = normalize(tok2[at].astype(F32))
        small[0:1] = small[0:1] + jnp.sum(g * n, axis=0, keepdims=True)
        resid[at] = box_gam[at] + norm_back(g * vecs[0:1], n, s)

    loop(length // rc, final_step)
    stores.append(pltpu.make_async_copy(resid, grad_tokens, out_sem.at[10]))
    stores.append(pltpu.make_async_copy(small, o_small, out_sem.at[11]))
    for cp in stores[-2:]:
        cp.start()
    for wait in pending:
        wait()
    act_swap.wait_send()
    gmix_swap.wait_send()
    gai_swap.wait_send()

    @pl.when(jnp.logical_not(last))
    def _():
        fore.wait_send()

    @pl.when(jnp.logical_not(first))
    def _():
        back.wait_send()

    for cp in stores:
        cp.wait()


COPIES = 5 * 12 + 2 * 14


def block_call(tokens, cot, w_in, w_out, w_gate, w_up, w_down, gains, taps):
    length, width = tokens.shape
    rows, ff = w_in.shape[0], w_gate.shape[1] // 2
    half = width // 2
    two = 2 * length
    hbm = pl.BlockSpec(memory_space=pltpu.HBM)
    vm = pl.BlockSpec(memory_space=pltpu.VMEM)

    def out(*shape, dtype=BF):
        return jax.ShapeDtypeStruct(shape, dtype)

    def mem(*shape, dtype=BF):
        return pltpu.VMEM(shape, dtype)

    dma = pltpu.SemaphoreType.DMA
    return pl.pallas_call(
        block_kernel,
        out_shape=(
            out(length, width), out(length, width, dtype=F32), out(two, width), out(two, width), out(two, ff),
            out(two, ff), out(two, ff), out(two, 3 * half), out(two, width), out(two, width), out(two, width),
            out(8, width, dtype=F32),
        ),
        in_specs=[hbm] * 7 + [vm] * 2,
        out_specs=(hbm,) * 12,
        scratch_shapes=[
            mem(8, rows, 3 * half), mem(8, rows, width), mem(2, 8, rows, ff), mem(8, rows, ff), mem(8, 32, 128),
            mem(two, width), mem(two, width), mem(two, width), mem(two, 3 * half, dtype=F32),
            mem(2, length + 8, half, dtype=F32), mem(two, half, dtype=F32), mem(two, width), mem(two, width, dtype=F32),
            mem(length, width, dtype=F32), mem(length, width, dtype=F32), mem(length, width, dtype=F32),
            mem(length, width, dtype=F32), mem(length, width, dtype=F32), mem(length, width, dtype=F32), mem(two, width),
            mem(two, ff), mem(two, ff, dtype=F32), mem(two, ff, dtype=F32), mem(two, ff), mem(two, ff), mem(two, width),
            mem(2, length + 8, half, dtype=F32), mem(two, 3 * half), mem(16, width, dtype=F32), mem(8, width, dtype=F32),
            mem(length, 128, dtype=F32), mem(length, width),
            dma((9,)), dma((COPIES,)), dma((COPIES,)), dma((len(SWAPS),)), dma((len(SWAPS),)), dma((12,)),
        ],
        compiler_params=pltpu.CompilerParams(collective_id=1, has_side_effects=True, vmem_limit_bytes=62 << 20),
    )(tokens, cot, w_in, w_out, w_gate, w_up, w_down, gains, taps)
ORDERS = ("XYZ", "YZX", "ZXY")
SIZES = {"X": (1, 4, 1, 4), "Y": (2, 1, 2, 4), "Z": (2, 4, 2, 1)}


def dims_left(order, phase):
    sizes = [2, 4, 2, 4]
    for axis in order[: phase + 1]:
        for i in {"X": (0, 2), "Y": (1,), "Z": (3,)}[axis]:
            sizes[i] = 1
    return tuple(n for n in sizes if n > 1)


def halves(columns):
    first = columns // 256 * 128
    return (0, first), (first, columns - first)


COUNT = 3
PLACES = 3 * COUNT


def reduce_kernel(*refs):
    n = COUNT
    ins, refs = refs[:10], refs[10:]
    outs, refs = refs[:6], refs[6:]
    held, refs = refs[:n], refs[n:]
    relay, refs = [refs[6 * t : 6 * t + 6] for t in range(n)], refs[6 * n :]
    takes, refs = [refs[6 * t : 6 * t + 6] for t in range(n)], refs[6 * n :]
    bufs, refs = refs[:10], refs[10:]
    turned, refs = refs[:4], refs[4:]
    local_sem, send_sem, recv_sem, spread_send, spread_recv, core_send, core_recv = refs
    o_gate, o_up, o_down, o_in, o_out, o_small = outs
    xl, xh, y, z, c = place()
    x = xh * 2 + xl
    loads = [pltpu.make_async_copy(a, b, local_sem.at[i]) for i, (a, b) in enumerate(zip(ins, bufs))]
    for cp in loads:
        cp.start()
    act_mid, gg, act_in, gproj, small, gu, gated, gmix, cot, hidden = bufs
    mid_t, in_t, gated_t, cot_t = turned
    half = gproj.shape[1] // 3
    ff = gg.shape[1]
    width = half * 2
    quarter = half // 2
    where = {"X": x, "Y": y, "Z": z}
    near = {
        "X": (device(x - 1, y, z, c), device(x + 1, y, z, c)),
        "Y": (device(x, y - 1, z, c), device(x, y + 1, z, c)),
        "Z": (device(x, y, z - 1, c), device(x, y, z + 1, c)),
    }
    replicas = [(dx, dz) for dx in (0, 2) for dz in (1, 3, 2, 0) if dx or dz]
    spread_to = [device(x + dx, y, z + dz, c) for dx, dz in replicas]
    sibling = device(x, y, z, 1 - c)
    far = [device(x + dx, y, z + dz, c) for dx, dz in replicas if (dx, dz) not in ((0, 1), (0, 3))]
    greet([*near["X"], *near["Y"], *near["Z"], *far, sibling])
    pending = []

    def index(order, phase, q):
        at = [slice(None)] * 4
        for a in order[:phase]:
            put(at, a, where[a])
        put(at, order[phase], q)
        return tuple(at)

    def put(at, axis, q):
        if axis == "X":
            at[0], at[2] = q % 2, q // 2
        else:
            at[1 if axis == "Y" else 3] = q

    def key(t, phase, k):
        return (t * 3 + phase) * 6 + k

    def ship(src, dst, to, t, phase, k):
        cp = remote(src, dst, send_sem.at[key(t, phase, k)], recv_sem.at[key(t, phase, k)], to)
        cp.start()
        pending.append(cp)

    def arrived(dst, t, phase, k):
        remote(dst, dst, send_sem.at[key(t, phase, k)], recv_sem.at[key(t, phase, k)], sibling).wait_recv()

    def cols(view, h, t):
        at, size = halves(held[t].shape[-1])[h]
        lead = len(view.shape) - 1
        return view.at[(slice(None),) * lead + (pl.ds(at, size),)]

    def part(ref, t, phase, q, h):
        return cols(ref.at[index(ORDERS[t], phase, q)], h, t)

    def buffers(t, phase):
        ra, rb = relay[t][2 * phase : 2 * phase + 2]
        tl, tr = takes[t][2 * phase : 2 * phase + 2]
        return ra, rb, tl, tr

    def each(dims, body):
        total = 1
        for d in dims:
            total *= d

        def step(i, carry):
            at, rest = [], i
            for d in reversed(dims):
                at.append(rest % d)
                rest = rest // d
            body(tuple(reversed(at)))
            return carry

        if total == 1:
            body(())
        else:
            lax.fori_loop(0, total, step, 0)

    def full(order, phase, q, at):
        idx, k = list(index(order, phase, q)), 0
        for i in range(4):
            if isinstance(idx[i], slice):
                idx[i] = at[k]
                k += 1
        return tuple(idx)

    def begin(t, phase, first=True, second=True):
        order = ORDERS[t]
        p = where[order[phase]]
        left, right = near[order[phase]]
        ra, rb, tl, tr = buffers(t, phase)
        src = held[t]
        far_q, next_q, last_q = (p + 2) % 4, (p + 1) % 4, (p + 3) % 4
        if first:
            ship(part(src, t, phase, far_q, 0), ra, right, t, phase, 0)
            ship(part(src, t, phase, far_q, 1), rb, left, t, phase, 1)
        if second:
            ship(part(src, t, phase, next_q, 1), cols(tl, 1, t), right, t, phase, 2)
            ship(part(src, t, phase, last_q, 0), cols(tr, 0, t), left, t, phase, 3)

    def middle(t, phase):
        order = ORDERS[t]
        p = where[order[phase]]
        left, right = near[order[phase]]
        ra, rb, tl, tr = buffers(t, phase)
        dims = dims_left(order, phase)
        for h, (box, q, to, dst) in enumerate(((ra, (p + 1) % 4, right, tl), (rb, (p + 3) % 4, left, tr))):
            arrived(box, t, phase, h)
            at0, size = halves(held[t].shape[-1])[h]

            def add(at, box=box, q=q, at0=at0, size=size):
                slab = full(order, phase, q, at) + (slice(None), pl.ds(at0, size))
                held[t][slab] = (held[t][slab].astype(F32) + box[at].astype(F32)).astype(BF)

            each(dims, add)
            ship(part(held[t], t, phase, q, h), cols(dst, h, t), to, t, phase, 4 + h)

    def finish(t, phase):
        order = ORDERS[t]
        p = where[order[phase]]
        ra, rb, tl, tr = buffers(t, phase)
        dims = dims_left(order, phase)
        arrived(cols(tl, 1, t), t, phase, 2)
        arrived(cols(tr, 0, t), t, phase, 3)
        arrived(cols(tl, 0, t), t, phase, 4)
        arrived(cols(tr, 1, t), t, phase, 5)

        def add(at):
            slab = full(order, phase, p, at)
            held[t][slab] = (held[t][slab].astype(F32) + tl[at].astype(F32) + tr[at].astype(F32)).astype(BF)

        each(dims, add)

    tile = 256

    def fill(t, step):
        axis = ORDERS[t][0]
        at = [slice(None)] * 4
        put(at, axis, (where[axis] + step) % 4)
        at = tuple(at)
        lead = dims_left(ORDERS[t], 0)

        def block(left, right, start, cols_n, put_at):
            rows = flat(left[at])

            def one(j):
                value = mul(rows, right[:, pl.ds(pl.multiple_of(start + j * tile, 128), tile)]).astype(BF)
                held[t][at + (slice(None), pl.ds(pl.multiple_of(put_at + j * tile, 128), tile))] = value.reshape(
                    lead + (16, tile)
                )

            loop(cols_n // tile, one)

        block((mid_t, mid_t, cot_t)[t], (gg, gu, hidden)[t], 0, ff, 0)
        block(in_t, gproj, t * half, half, ff)
        if t:
            block(gated_t, gmix, c * half + (t - 1) * quarter, quarter, ff + half)

    def turn(source, target):
        size = 128

        def one(i):
            target[:, :, :, :, :, chunk(i, size)] = source[chunk(i, size)].T.reshape(target.shape[:5] + (size,))

        loop(source.shape[0] // size, one)

    for cp in loads[:5]:
        cp.wait()
    tall = jnp.concatenate([small[...], jnp.zeros((120, width), F32)], axis=0)
    held[0][:, :, :, :, :, pl.ds(ff + half, 128)] = tall.T.astype(BF).reshape(2, 4, 2, 4, 16, 128)
    turn(act_mid, mid_t)
    turn(act_in, in_t)
    fill(0, 2)
    begin(0, 0, second=False)
    for cp in loads[5:8]:
        cp.wait()
    turn(gated, gated_t)
    fill(1, 2)
    begin(1, 0, second=False)
    for cp in loads[8:]:
        cp.wait()
    turn(cot, cot_t)
    fill(2, 2)
    begin(2, 0, second=False)
    for t in range(n):
        fill(t, 1)
        fill(t, 3)
        begin(t, 0, first=False)
    for t in range(n):
        fill(t, 0)
    for phase in range(3):
        if phase:
            for t in range(n):
                begin(t, phase)
        for t in range(n):
            middle(t, phase)
        for t in range(n):
            finish(t, phase)
    pieces = (
        ((0, ff, o_gate, c * ff), (ff, half, o_in, c * half), (ff + half, 128, o_small, c * 128)),
        ((0, ff, o_up, c * ff), (ff, half, o_in, width + c * half), (ff + half, quarter, o_out, c * half)),
        ((0, ff, o_down, c * ff), (ff, half, o_in, 2 * width + c * half), (ff + half, quarter, o_out, c * half + quarter)),
    )
    other = (
        ((o_gate, (1 - c) * ff), (o_in, (1 - c) * half), (o_small, (1 - c) * 128)),
        ((o_up, (1 - c) * ff), (o_in, width + (1 - c) * half), (o_out, (1 - c) * half)),
        ((o_down, (1 - c) * ff), (o_in, 2 * width + (1 - c) * half), (o_out, (1 - c) * half + quarter)),
    )
    slot = xh * 4 + z

    def spot(out, row, count, col, size):
        return out.at[pl.ds(pl.multiple_of(row, 16), count), pl.ds(pl.multiple_of(col, 128), size)]

    keeps = []
    for t in range(n):
        for k, (at, size, out, col) in enumerate(pieces[t]):
            piece = held[t].at[xl, y, xh, z, :, pl.ds(at, size)]
            dst = spot(out, slot * 16, 16, col, size)
            for i, to in enumerate(spread_to):
                key_ = (t * 3 + k) * 7 + i
                cp = remote(piece, dst, spread_send.at[key_], spread_recv.at[key_], to)
                cp.start()
                pending.append(cp)
            keeps.append(pltpu.make_async_copy(piece, dst, local_sem.at[t * 3 + k]))
            keeps[-1].start()
    for t in range(n):
        for k, (at, size, out, col) in enumerate(pieces[t]):
            keeps[t * 3 + k].wait()
            for i, (dx, dz) in enumerate(replicas):
                src = ((xh + dx // 2) % 2) * 4 + (z + 4 - dz) % 4
                dst = spot(out, src * 16, 16, col, size)
                key_ = (t * 3 + k) * 7 + i
                remote(dst, dst, spread_send.at[key_], spread_recv.at[key_], sibling).wait_recv()
            whole = spot(out, 0, 128, col, size)
            cp = remote(whole, whole, core_send.at[t * 3 + k], core_recv.at[t * 3 + k], sibling)
            cp.start()
            pending.append(cp)
    for t in range(n):
        for k, (out, col) in enumerate(other[t]):
            dst = spot(out, 0, 128, col, pieces[t][k][1])
            remote(dst, dst, core_send.at[t * 3 + k], core_recv.at[t * 3 + k], sibling).wait_recv()
    for cp in pending:
        cp.wait_send()


def reduce_grads(act_mid, gg, act_in, gproj, small, gu, gated, gmix, cot, hidden):
    n = COUNT
    ins = (act_mid, gg, act_in, gproj, small, gu, gated, gmix, cot, hidden)
    width, ff, two = act_in.shape[1], gg.shape[1], act_in.shape[0]
    half = width // 2
    widths = (ff + half + 128, ff + half + half // 2, ff + half + half // 2)
    lead = (2, 4, 2, 4, 16)
    held = [pltpu.VMEM(lead + (w,), BF) for w in widths]
    relay, takes = [], []
    for t in range(n):
        for phase in range(3):
            dims = dims_left(ORDERS[t], phase)
            for h in (0, 1):
                relay.append(pltpu.VMEM(dims + (16, halves(widths[t])[h][1]), BF))
                takes.append(pltpu.VMEM(dims + (16, widths[t]), BF))
    bufs = [pltpu.VMEM(a.shape, a.dtype) for a in ins]
    turned = [pltpu.VMEM(lead + (two,), BF)] * 4
    dma = pltpu.SemaphoreType.DMA
    hbm = pl.BlockSpec(memory_space=pltpu.HBM)
    rows = 128
    outs = (2 * ff, 2 * ff, 2 * ff, 3 * width, width, 256)
    return pl.pallas_call(
        reduce_kernel,
        out_shape=tuple(jax.ShapeDtypeStruct((rows, w), BF) for w in outs),
        in_specs=[hbm] * len(ins),
        out_specs=(hbm,) * len(outs),
        scratch_shapes=held + relay + takes + bufs + turned
        + [dma((10,)), dma((54,)), dma((54,)), dma((63,)), dma((63,)), dma((9,)), dma((9,))],
        compiler_params=pltpu.CompilerParams(collective_id=2, has_side_effects=True, vmem_limit_bytes=62 << 20),
    )(*ins)


def local(tokens, norm_in, w_in, conv_w, w_out, norm_mid, w_gate, w_up, w_down, cotangent):
    gains = jnp.stack([norm_in, norm_mid])
    (
        result, grad_tokens, act_in, act_mid, hidden, gg, gu, gproj, gated, gmix, cot, small
    ) = block_call(tokens[0], cotangent[0], w_in, w_out, w_gate, w_up, w_down, gains, conv_w.T)
    sums = reduce_grads(act_mid, gg, act_in, gproj, small, gu, gated, gmix, cot, hidden)
    g_gate, g_up, g_down, g_in, g_out, g_small = (s.astype(F32) for s in sums)
    g_small = g_small[:, :128] + g_small[:, 128:]
    return (
        result[None],
        grad_tokens[None],
        g_small[:, 0],
        g_in,
        g_small[:, 2:5],
        g_out,
        g_small[:, 1],
        g_gate,
        g_up,
        g_down,
    )


def solution(mesh):
    row, act, vec = P("shard", None), P("replica", "shard", None), P("shard")
    in_specs = (act, vec, row, row, row, vec, row, row, row, act)
    out_specs = (act, act, vec, row, row, row, vec, row, row, row)
    return jax.shard_map(local, mesh=mesh, in_specs=in_specs, out_specs=out_specs, check_vma=False)
```

```python
import jax
import jax.numpy as jnp
from jax import lax
from jax.sharding import PartitionSpec as P
from jax.experimental import pallas as pl
from jax.experimental.pallas import tpu as pltpu

MESH = pl.DeviceIdType.MESH
BF = jnp.bfloat16
F32 = jnp.float32
EPS = 1e-05


def place():
    s = lax.axis_index("shard")
    r = lax.axis_index("replica")
    xl, y = s // 4, s % 4
    z, xh, c = r // 4, (r // 2) % 2, r % 2
    return xl, xh, y, z, c


def device(x, y, z, c):
    x, y, z = (x + 4) % 4, (y + 4) % 4, (z + 4) % 4
    return ((x % 2) * 4 + y, z * 4 + (x // 2) * 2 + c)


def remote(src, dst, send, recv, to):
    return pltpu.make_async_remote_copy(
        src_ref=src, dst_ref=dst, send_sem=send, recv_sem=recv, device_id=to, device_id_type=MESH
    )


def greet(devices):
    barrier = pltpu.get_barrier_semaphore()
    for to in devices:
        pl.semaphore_signal(barrier, inc=1, device_id=to, device_id_type=MESH)
    pl.semaphore_wait(barrier, len(devices))


def mul(left, right):
    return lax.dot_general(left, right, (((1,), (0,)), ((), ())), preferred_element_type=F32)


def times_rows(left, right):
    return lax.dot_general(left, right, (((1,), (1,)), ((), ())), preferred_element_type=F32)


def normalize(values):
    scale = lax.rsqrt(jnp.mean(values * values, axis=-1, keepdims=True) + EPS)
    return values * scale, scale


def norm_back(grad_normed, normed, scale):
    return scale * (grad_normed - normed * jnp.mean(grad_normed * normed, axis=-1, keepdims=True))


def loop(count, body):
    def step(i, carry):
        body(i)
        return carry

    lax.fori_loop(0, count, step, 0)


def chunk(i, size):
    return pl.ds(pl.multiple_of(i * size, size), size)


def flat(value):
    return value.reshape(-1, value.shape[-1])


ORDERS = ("XYZ", "YZX", "ZXY") * 2
SIZES = {"X": (1, 4, 1, 4), "Y": (2, 1, 2, 4), "Z": (2, 4, 2, 1)}


def dims_left(order, phase):
    sizes = [2, 4, 2, 4]
    for axis in order[: phase + 1]:
        for i in {"X": (0, 2), "Y": (1,), "Z": (3,)}[axis]:
            sizes[i] = 1
    return tuple(n for n in sizes if n > 1)


def halves(columns):
    first = columns // 256 * 128
    return (0, first), (first, columns - first)


EARLY = 1536
WIDE = 768
LEAD = (2, 4, 2, 4, 16)


def put(at, axis, q):
    if axis == "X":
        at[0], at[2] = q % 2, q // 2
    else:
        at[1 if axis == "Y" else 3] = q


def quarter_at(axis, q):
    at = [slice(None)] * 4
    put(at, axis, q)
    return tuple(at)


def turn(source, target):
    size = 128

    def one(i):
        target[:, :, :, :, :, chunk(i, size)] = source[chunk(i, size)].T.reshape(LEAD + (size,))

    loop(source.shape[0] // size, one)


SWAPS = ("tokens", "cot", "gated0", "gated1", "mix", "act", "ffn", "gam", "gmix", "gai", "fore", "back")
TILE = 256


def block_kernel(
    tokens, cot, w_in, w_out, w_gate, w_up, w_down, gains, taps_in,
    result, grad_tokens, o_in_t, o_mid_t, o_hidden, o_gg, o_gu, o_proj, o_gated, o_mix, o_cot_t, o_small,
    own0, left0, right0, own1, left1, right1, own2, left2, right2,
    win, wout, wgu, wd, ext, tok2, cot2, act_in, proj, mixed, conv, gated, part, box_mix, box_ffn, box_gam, box_gai,
    resid, normed, act_mid, hidden, held, gg, gu, gmix, gconv, gproj, vecs, small, scale_mid, out_res, mid_t, cot_t,
    far_a0, far_b0, far_a1, far_b1, far_a2, far_b2,
    local_sem, send_sem, recv_sem, core_send, core_recv, out_sem, early_send, early_recv,
):
    xl, xh, y, z, c = place()
    x = xh * 2 + xl
    shard, replica = lax.axis_index("shard"), lax.axis_index("replica")
    own = xl * 4 + y
    length, width = tokens.shape
    half = width // 2
    ff = wd.shape[2]
    rows = wd.shape[1]
    mine = z % 2
    xp, xm = device(x + 1, y, z, c), device(x - 1, y, z, c)
    yp, ym = device(x, y + 1, z, c), device(x, y - 1, z, c)
    zp, zm = device(x, y, z + 1, c), device(x, y, z - 1, c)
    sibling = device(x, y, z, 1 - c)
    nxt, prv = ((shard + 1) % 8, replica), ((shard + 7) % 8, replica)
    first, last = shard == 0, shard == 7

    ext[own] = jnp.concatenate([gains[...].astype(F32), taps_in[...].astype(F32), jnp.zeros((27, 128), F32)], axis=0).astype(BF)
    copies = []
    for i in range(3):
        copies.append((w_in.at[:, pl.ds(pl.multiple_of(i * width + c * half, 128), half)], win.at[own, :, pl.ds(i * half, half)]))
    copies.append((w_gate.at[:, pl.ds(pl.multiple_of(c * ff, 128), ff)], wgu.at[0, own]))
    copies.append((w_up.at[:, pl.ds(pl.multiple_of(c * ff, 128), ff)], wgu.at[1, own]))
    copies.append((w_out, wout.at[own]))
    copies.append((w_down.at[:, pl.ds(pl.multiple_of(c * ff, 128), ff)], wd.at[own]))
    copies.append((tokens, tok2.at[pl.ds(0, length)]))
    copies.append((cot, cot2.at[pl.ds(0, length)]))
    loads = [pltpu.make_async_copy(a, b, local_sem.at[i]) for i, (a, b) in enumerate(copies)]
    for cp in loads:
        cp.start()
    greet([xp, xm, yp, ym, zp, zm, sibling, nxt, prv])

    pending, stores, used = [], [], []

    def store(src, dst):
        stores.append(pltpu.make_async_copy(src, dst, out_sem.at[len(used)]))
        used.append(dst)
        stores[-1].start()

    def fire(cp):
        cp.start()
        pending.append(cp.wait_send)

    def swap(name, src, dst, to=None):
        k = SWAPS.index(name)
        return remote(src, dst, core_send.at[k], core_recv.at[k], sibling if to is None else to)

    def wd_part(g, u):
        return wd.at[u, pl.ds(pl.multiple_of(g * (rows // 4), rows // 4), rows // 4)]

    parts = [
        (lambda g, u: ext.at[u], False),
        (lambda g, u: win.at[u], False),
        (lambda g, u: wgu.at[g, u], True),
        (lambda g, u: wout.at[u], False),
        (wd_part, True),
        (lambda g, u: wd.at[u, pl.ds(rows // 2, rows // 2)], False),
    ]
    keys, count = {}, 0
    for p in range(len(parts)):
        names = ["y+", "y-", "f+", "f-"]
        for dy in (0, -1, 1, 2):
            for h in (0, 1):
                names.append(("x", dy, h))
                if parts[p][1]:
                    names.append(("z", 1, dy, h))
                    if dy:
                        names.append(("z", 0, dy, h))
        for name in names:
            keys[p, name] = count
            count += 1
    assert count == COPIES

    def send(view, to, k):
        fire(remote(view, view, send_sem.at[k], recv_sem.at[k], to))

    def got(view, k):
        remote(view, view, send_sem.at[k], recv_sem.at[k], yp).wait_recv()

    def cut(view, h):
        hr = view.shape[0] // 2
        return view.at[pl.ds(h * hr, hr)]

    def at_y(dy):
        return xl * 4 + (y + dy + 4) % 4

    def over(dy):
        return (1 - xl) * 4 + (y + dy + 4) % 4

    def send_x(p, dy, h):
        send(cut(parts[p][0](mine, at_y(dy)), h), (xp, xm)[h], keys[p, ("x", dy, h)])

    def send_z(p, other, dy, h):
        if parts[p][1]:
            u = over(dy) if other else at_y(dy)
            send(cut(parts[p][0](mine, u), h), (zp, zm)[h], keys[p, ("z", other, dy, h)])

    def launch_y(p):
        view = parts[p][0]
        send(view(mine, own), yp, keys[p, "y+"])
        send(view(mine, own), ym, keys[p, "y-"])

    def launch_x(p):
        for h in (0, 1):
            send_x(p, 0, h)

    def stage_a(p):
        view = parts[p][0]
        got(view(mine, at_y(-1)), keys[p, "y+"])
        send(cut(view(mine, at_y(-1)), 0), yp, keys[p, "f+"])
        for h in (0, 1):
            send_z(p, 0, -1, h)
            send_x(p, -1, h)
        got(view(mine, at_y(1)), keys[p, "y-"])
        send(cut(view(mine, at_y(1)), 1), ym, keys[p, "f-"])
        for h in (0, 1):
            send_z(p, 0, 1, h)
            send_x(p, 1, h)

    def stage_b(p):
        view = parts[p][0]
        for h in (0, 1):
            got(cut(view(mine, at_y(2)), h), keys[p, ("f+", "f-")[h]])
            send_z(p, 0, 2, h)
            send_x(p, 2, h)

    def stage_c(p, *dys):
        view = parts[p][0]
        for dy in dys or (0, -1, 1, 2):
            for h in (0, 1):
                got(cut(view(mine, over(dy)), h), keys[p, ("x", dy, h)])
                send_z(p, 1, dy, h)

    def stage_d(p):
        view = parts[p][0]
        for h in (0, 1):
            for dy in (0, -1, 1, 2):
                if dy:
                    got(cut(view(1 - mine, at_y(dy)), h), keys[p, ("z", 0, dy, h)])
                got(cut(view(1 - mine, over(dy)), h), keys[p, ("z", 1, dy, h)])

    EXT, WIN, WGU, WOUT, WDZ, WDX = range(6)
    lower, upper = pl.ds(0, length), pl.ds(length, length)
    launch_y(EXT)
    launch_x(EXT)
    for cp in loads[3:5]:
        cp.wait()
    launch_y(WGU)
    launch_x(WGU)
    for cp in loads[:3]:
        cp.wait()
    launch_y(WIN)
    launch_x(WIN)
    for cp in loads[7:]:
        cp.wait()
    fire(swap("tokens", tok2.at[lower], tok2.at[upper]))
    fire(swap("cot", cot2.at[lower], cot2.at[upper]))
    for cp in loads[5:7]:
        cp.wait()
    launch_x(WOUT)
    launch_x(WDZ)
    launch_x(WDX)
    for stage in (stage_a, stage_b, stage_c):
        stage(EXT)
    for u in range(8):
        vecs[:, pl.ds(u * 128, 128)] = ext[u, pl.ds(0, 16)].astype(F32)
    small[...] = jnp.zeros_like(small)
    mixed[:, pl.ds(0, 8)] = jnp.zeros((2, 8, half), F32)
    gconv[:, pl.ds(length, 8)] = jnp.zeros((2, 8, half), F32)
    swap("tokens", tok2.at[lower], tok2.at[upper]).wait_recv()
    rc = 32

    def norm_in_step(i):
        v, _ = normalize(tok2[chunk(i, rc)].astype(F32))
        act_in[chunk(i, rc)] = (v * vecs[0:1]).astype(BF)

    loop(2 * length // rc, norm_in_step)
    turn(act_in, mid_t)
    store(mid_t, o_in_t)
    in_store = stores.pop()
    stage_c(WGU, 0)
    stage_a(WGU)
    launch_y(WOUT)
    stage_a(WIN)
    launch_y(WDZ)
    stage_c(WGU, -1, 1)
    stage_b(WGU)
    stage_a(WOUT)
    launch_y(WDX)
    stage_b(WIN)
    stage_c(WGU, 2)
    stage_a(WDZ)
    swap("cot", cot2.at[lower], cot2.at[upper]).wait_recv()
    turn(cot2, cot_t)
    store(cot_t, o_cot_t)
    stage_c(WIN)

    def proj_step(j):
        proj[:, chunk(j, TILE)] = mul(act_in[...], flat(win[:, :, chunk(j, TILE)]))

    loop(3 * half // TILE, proj_step)

    def b_of(at):
        return proj[at, pl.ds(0, half)]

    def c_of(at):
        return proj[at, pl.ds(half, half)]

    def x_of(at):
        return proj[at, pl.ds(2 * half, half)]

    def mixed_step(i):
        for q in (0, 1):
            at = pl.ds(pl.multiple_of(q * length + i * rc, rc), rc)
            mixed[q, pl.ds(pl.multiple_of(8 + i * rc, 8), rc)] = (b_of(at) * x_of(at)).astype(BF).astype(F32)

    loop(length // rc, mixed_step)
    fore = swap("fore", mixed.at[:, pl.ds(length, 8)], mixed.at[:, pl.ds(0, 8)], nxt)
    back = swap("back", gconv.at[:, pl.ds(0, 8)], gconv.at[:, pl.ds(length, 8)], prv)

    @pl.when(jnp.logical_not(last))
    def _():
        fore.start()

    stage_b(WOUT)
    stage_c(WDZ, 0)
    stage_a(WDX)

    @pl.when(jnp.logical_not(first))
    def _():
        fore.wait_recv()

    taps = [vecs[pl.ds(2 + k, 1), pl.ds(pl.multiple_of(c * half, 128), half)] for k in range(3)]
    rq = 64

    def conv_step(i):
        for q in (0, 1):
            window = mixed[q, pl.ds(pl.multiple_of(i * rq, 8), rq + 8)]
            value = taps[0] * window[6 : 6 + rq] + taps[1] * window[7 : 7 + rq] + taps[2] * window[8 : 8 + rq]
            at = pl.ds(pl.multiple_of(q * length + i * rq, rq), rq)
            conv[at] = value
            gated[at, pl.ds(pl.multiple_of(c * half, 128), half)] = (c_of(at) * value).astype(BF)

    loop(length // rq, conv_step)
    gated_mine = gated.at[:, pl.ds(pl.multiple_of(c * half, 128), half)]
    gated_other = gated.at[:, pl.ds(pl.multiple_of((1 - c) * half, 128), half)]
    fire(swap("gated0", gated_mine.at[lower], gated_mine.at[upper]))
    fire(swap("gated1", gated_mine.at[upper], gated_mine.at[lower]))
    stage_b(WDZ)
    stage_c(WDZ, -1, 1)
    stage_c(WOUT)
    wout_mine = wout.at[pl.ds(pl.multiple_of(c * 4, 4), 4)]

    def mix_step(j):
        part[:, chunk(j, TILE)] = mul(gated_mine[...], flat(wout_mine[:, :, chunk(j, TILE)]))

    loop(width // TILE, mix_step)
    mix_swap = swap("mix", part.at[upper], box_mix)
    mix_swap.start()
    stage_b(WDX)
    mix_swap.wait_recv()

    def norm_mid_step(i):
        at = chunk(i, rc)
        v = tok2[at].astype(F32) + part[at] + box_mix[at]
        n, s = normalize(v)
        resid[at] = v
        normed[at] = n
        scale_mid[at] = jnp.broadcast_to(s, (rc, 128))
        act_mid[at] = (n * vecs[1:2]).astype(BF)

    loop(length // rc, norm_mid_step)
    act_swap = swap("act", act_mid.at[lower], act_mid.at[upper])
    act_swap.start()
    stage_c(WDZ, 2)
    act_swap.wait_recv()
    in_store.wait()
    turn(act_mid, mid_t)
    store(mid_t, o_mid_t)
    stage_d(WGU)

    where = {"X": x, "Y": y, "Z": z}
    near = {"X": (xm, xp), "Y": (ym, yp), "Z": (zm, zp)}
    landings = ((own0, left0, right0), (own1, left1, right1), (own2, left2, right2))
    relays = ((far_a0, far_b0), (far_a1, far_b1), (far_a2, far_b2))
    eh = EARLY // 2

    def early_at(t, step):
        axis = ORDERS[t][0]
        return quarter_at(axis, (where[axis] + step) % 4)

    def early_fill(t, step):
        at = early_at(t, step)
        lead = dims_left(ORDERS[t], 0) + (16, WIDE)
        tall, right = flat((mid_t, mid_t, cot_t)[t][at]), (gg, gu, hidden)[t]

        def one(j):
            value = mul(tall, right[:, chunk(j, WIDE)]).astype(BF)
            held[(t,) + at + (slice(None), chunk(j, WIDE))] = value.reshape(lead)

        loop(EARLY // WIDE, one)

    def early_cols(view, h):
        return view.at[(slice(None),) * (len(view.shape) - 1) + (pl.ds(h * eh, eh),)]

    def early_copy(t, k):
        to_right = k in (0, 2, 4)
        h = (0, 1, 1, 0, 0, 1)[k]
        step = 2 if k < 2 else (1 if to_right else 3)
        src = early_cols(held.at[(t,) + early_at(t, step)], h)
        dst = relays[t][k] if k < 2 else early_cols(landings[t][1 if to_right else 2], h)
        to = near[ORDERS[t][0]][1 if to_right else 0]
        return remote(src, dst, early_send.at[t * 6 + k], early_recv.at[t * 6 + k], to)

    def gate_step(j):
        at = chunk(j, TILE)
        gate = mul(act_mid[...], flat(wgu[0, :, :, at]))
        up = mul(act_mid[...], flat(wgu[1, :, :, at]))
        sig = jax.nn.sigmoid(gate)
        silu = gate * sig
        hidden[:, at] = (silu * up).astype(BF)
        factor = up * (sig * (1.0 + gate * (1.0 - sig)))
        spot = (slice(None),) * 4 + (chunk(j % 6, TILE),)
        held[(j // 6, 0) + spot] = factor.astype(BF).reshape(LEAD[1:] + (TILE,))
        held[(j // 6, 1) + spot] = silu.astype(BF).reshape(LEAD[1:] + (TILE,))

    loop(ff // TILE, gate_step)
    store(hidden, o_hidden)
    early_fill(2, 2)
    fire(early_copy(2, 0))
    fire(early_copy(2, 1))
    early_fill(2, 1)
    fire(early_copy(2, 2))
    early_fill(2, 3)
    fire(early_copy(2, 3))
    early_fill(2, 0)
    store(held.at[(2,) + early_at(2, 0)], landings[2][0])
    stage_c(WDX)
    stage_d(WDZ)

    def grad_hidden_step(j):
        at = chunk(j, TILE)
        g = mul(cot2[...], flat(wd[:, :, at]))
        spot = (slice(None),) * 4 + (chunk(j % 6, TILE),)
        gg[:, at] = (g * flat(held[(j // 6, 0) + spot]).astype(F32)).astype(BF)
        gu[:, at] = (g * flat(held[(j // 6, 1) + spot]).astype(F32)).astype(BF)

    loop(ff // TILE, grad_hidden_step)
    store(gg, o_gg)
    store(gu, o_gu)
    for t in (0, 1):
        early_fill(t, 2)
        fire(early_copy(t, 0))
        fire(early_copy(t, 1))
    for t in (0, 1):
        early_fill(t, 1)
        fire(early_copy(t, 2))
    swap("mix", part.at[upper], box_mix).wait_send()

    def gam_step(j):
        u = pl.ds(j * 2, 2)
        part[:, chunk(j, TILE)] = times_rows(gg[...], flat(wgu[0, u])) + times_rows(gu[...], flat(wgu[1, u]))

    loop(4, gam_step)
    gam_swap = swap("gam", part.at[upper], box_gam)
    gam_swap.start()
    for t in (0, 1):
        early_fill(t, 3)
        fire(early_copy(t, 3))
    gam_swap.wait_recv()

    def resid_step(i):
        at = chunk(i, rc)
        g = part[at] + box_gam[at]
        n = normed[at]
        small[1:2] = small[1:2] + jnp.sum(g * n, axis=0, keepdims=True)
        full = cot2[at].astype(F32) + norm_back(g * vecs[1:2], n, scale_mid[at, 0:1])
        box_gam[at] = full
        gmix[at] = full.astype(BF)

    loop(length // rc, resid_step)
    gmix_swap = swap("gmix", gmix.at[lower], gmix.at[upper])
    gmix_swap.start()
    for t in (0, 1):
        early_fill(t, 0)
        store(held.at[(t,) + early_at(t, 0)], landings[t][0])
    gam_swap.wait_send()

    def ffn_step(j):
        u = pl.ds(j * 2, 2)
        part[:, chunk(j, TILE)] = times_rows(hidden[...], flat(wd[u]))

    loop(4, ffn_step)
    for t in range(3):
        for k in (0, 1):
            early_copy(t, k).wait_recv()
            at = early_at(t, (1, 3)[k])
            box = relays[t][k]
            dims = dims_left(ORDERS[t], 0)
            total = dims[0] * dims[1] * (dims[2] if len(dims) > 2 else 1)

            def add(i, at=at, box=box, dims=dims, t=t, k=k):
                places, rest = [], i
                for d in reversed(dims):
                    places.append(rest % d)
                    rest = rest // d
                places = tuple(reversed(places))
                left_over = iter(places)
                spot = (t,) + tuple(next(left_over) if isinstance(a, slice) else a for a in at)
                spot = spot + (slice(None), pl.ds(k * eh, eh))
                held[spot] = (held[spot].astype(F32) + box[places].astype(F32)).astype(BF)

            loop(total, add)
            fire(early_copy(t, 4 + k))
    ffn_swap = swap("ffn", part.at[upper], box_ffn)
    ffn_swap.start()

    def own_ffn_step(i):
        at = chunk(i, rc)
        resid[at] = resid[at] + part[at]

    loop(length // rc, own_ffn_step)
    gmix_swap.wait_recv()
    for q in (0, 1):
        box_mix[:, pl.ds(q * half, half)] = times_rows(gmix[pl.ds(q * length, length)], flat(wout_mine[...]))

    def gconv_step(i):
        for q in (0, 1):
            at = pl.ds(pl.multiple_of(q * length + i * rc, rc), rc)
            window = mixed[q, pl.ds(pl.multiple_of(i * rc, 8), rc + 8)]
            g = box_mix[pl.ds(pl.multiple_of(i * rc, rc), rc), pl.ds(q * half, half)]
            gc = g * c_of(at)
            gconv[q, pl.ds(pl.multiple_of(i * rc, 8), rc)] = gc
            gproj[at, pl.ds(half, half)] = (g * conv[at]).astype(BF)
            for k in range(3):
                spot = (pl.ds(2 + k, 1), pl.ds(pl.multiple_of(c * half, 128), half))
                small[spot] = small[spot] + jnp.sum(gc * window[6 + k : 6 + k + rc], axis=0, keepdims=True)

    loop(length // rc, gconv_step)

    @pl.when(jnp.logical_not(first))
    def _():
        back.start()

    @pl.when(jnp.logical_not(last))
    def _():
        back.wait_recv()

    def gproj_step(i):
        for q in (0, 1):
            at = pl.ds(pl.multiple_of(q * length + i * rc, rc), rc)
            window = gconv[q, pl.ds(pl.multiple_of(i * rc, 8), rc + 8)]
            gm = taps[2] * window[0:rc] + taps[1] * window[1 : rc + 1] + taps[0] * window[2 : rc + 2]
            gproj[at, pl.ds(0, half)] = (gm * x_of(at)).astype(BF)
            gproj[at, pl.ds(2 * half, half)] = (gm * b_of(at)).astype(BF)

    loop(length // rc, gproj_step)
    ffn_swap.wait_send()

    def gai_step(j):
        u = pl.ds(j * 2, 2)
        part[:, chunk(j, TILE)] = times_rows(gproj[...], flat(win[u]))

    loop(4, gai_step)
    gai_swap = swap("gai", part.at[upper], box_gai)
    gai_swap.start()
    ffn_swap.wait_recv()

    def result_step(i):
        at = chunk(i, rc)
        out_res[at] = (resid[at] + box_ffn[at]).astype(BF)

    loop(length // rc, result_step)
    swap("gated0", gated_other.at[upper], gated_other.at[upper]).wait_recv()
    swap("gated1", gated_other.at[lower], gated_other.at[lower]).wait_recv()
    store(gproj, o_proj)
    store(gated, o_gated)
    store(gmix, o_mix)
    store(out_res, result)
    gai_swap.wait_recv()

    def final_step(i):
        at = chunk(i, rc)
        g = part[at] + box_gai[at]
        n, s = normalize(tok2[at].astype(F32))
        small[0:1] = small[0:1] + jnp.sum(g * n, axis=0, keepdims=True)
        resid[at] = box_gam[at] + norm_back(g * vecs[0:1], n, s)

    loop(length // rc, final_step)
    store(resid, grad_tokens)
    store(small, o_small)
    for t in range(3):
        for k in (2, 3, 4, 5):
            early_copy(t, k).wait_recv()
    for wait in pending:
        wait()
    act_swap.wait_send()
    gmix_swap.wait_send()
    gai_swap.wait_send()

    @pl.when(jnp.logical_not(last))
    def _():
        fore.wait_send()

    @pl.when(jnp.logical_not(first))
    def _():
        back.wait_send()

    for cp in stores:
        cp.wait()


COPIES = 6 * 12 + 2 * 14


def block_call(tokens, cot, w_in, w_out, w_gate, w_up, w_down, gains, taps):
    length, width = tokens.shape
    rows, ff = w_in.shape[0], w_gate.shape[1] // 2
    half = width // 2
    two = 2 * length
    hbm = pl.BlockSpec(memory_space=pltpu.HBM)
    vm = pl.BlockSpec(memory_space=pltpu.VMEM)

    def out(*shape, dtype=BF):
        return jax.ShapeDtypeStruct(shape, dtype)

    def mem(*shape, dtype=BF):
        return pltpu.VMEM(shape, dtype)

    firsts = [dims_left(ORDERS[t], 0) + (16,) for t in range(3)]
    early = [out(*firsts[t], EARLY) for t in range(3) for _ in range(3)]
    relays = [mem(*firsts[t], EARLY // 2) for t in range(3) for _ in range(2)]
    dma = pltpu.SemaphoreType.DMA
    return pl.pallas_call(
        block_kernel,
        out_shape=(
            out(length, width), out(length, width, dtype=F32), out(*LEAD, two), out(*LEAD, two), out(two, ff),
            out(two, ff), out(two, ff), out(two, 3 * half), out(two, width), out(two, width), out(*LEAD, two),
            out(8, width, dtype=F32), *early,
        ),
        in_specs=[hbm] * 7 + [vm] * 2,
        out_specs=(hbm,) * 21,
        scratch_shapes=[
            mem(8, rows, 3 * half), mem(8, rows, width), mem(2, 8, rows, ff), mem(8, rows, ff), mem(8, 32, 128),
            mem(two, width), mem(two, width), mem(two, width), mem(two, 3 * half, dtype=F32),
            mem(2, length + 8, half, dtype=F32), mem(two, half, dtype=F32), mem(two, width), mem(two, width, dtype=F32),
            mem(length, width, dtype=F32), mem(length, width, dtype=F32), mem(length, width, dtype=F32),
            mem(length, width, dtype=F32), mem(length, width, dtype=F32), mem(length, width, dtype=F32), mem(two, width),
            mem(two, ff), mem(3, *LEAD, EARLY), mem(two, ff), mem(two, ff), mem(two, width),
            mem(2, length + 8, half, dtype=F32), mem(two, 3 * half), mem(16, width, dtype=F32), mem(8, width, dtype=F32),
            mem(length, 128, dtype=F32), mem(length, width), mem(*LEAD, two), mem(*LEAD, two), *relays,
            dma((9,)), dma((COPIES,)), dma((COPIES,)), dma((len(SWAPS),)), dma((len(SWAPS),)), dma((15,)), dma((18,)), dma((18,)),
        ],
        compiler_params=pltpu.CompilerParams(collective_id=1, has_side_effects=True, vmem_limit_bytes=62 << 20),
    )(tokens, cot, w_in, w_out, w_gate, w_up, w_down, gains, taps)
COUNT = 6


def reduce_kernel(*refs):
    n = COUNT
    ins, refs = refs[:10], refs[10:]
    begun, refs = refs[:9], refs[9:]
    outs, refs = refs[:6], refs[6:]
    held, refs = refs[:n], refs[n:]
    relay, refs = [refs[6 * t : 6 * t + 6] for t in range(n)], refs[6 * n :]
    takes, refs = [refs[6 * t : 6 * t + 6] for t in range(n)], refs[6 * n :]
    bufs, refs = refs[:10], refs[10:]
    turned, refs = refs[:1], refs[1:]
    local_sem, send_sem, recv_sem, spread_send, spread_recv, core_send, core_recv = refs
    o_gate, o_up, o_down, o_in, o_out, o_small = outs
    xl, xh, y, z, c = place()
    x = xh * 2 + xl
    loads = [pltpu.make_async_copy(a, b, local_sem.at[i]) for i, (a, b) in enumerate(zip(ins, bufs))]
    mid_t, gg, in_t, gproj, small, gu, gated, gmix, cot_t, hidden = bufs
    (gated_t,) = turned
    half = gproj.shape[1] // 3
    ff = gg.shape[1]
    width = half * 2
    quarter = half // 2
    where = {"X": x, "Y": y, "Z": z}
    near = {
        "X": (device(x - 1, y, z, c), device(x + 1, y, z, c)),
        "Y": (device(x, y - 1, z, c), device(x, y + 1, z, c)),
        "Z": (device(x, y, z - 1, c), device(x, y, z + 1, c)),
    }
    taken = []
    for t in range(3):
        at = quarter_at(ORDERS[t][0], where[ORDERS[t][0]])
        boxes = (held[t].at[at], takes[t][0], takes[t][1])
        taken += [pltpu.make_async_copy(begun[3 * t + k], boxes[k], local_sem.at[10 + 3 * t + k]) for k in range(3)]
    for cp in (*loads, *taken):
        cp.start()
    across, beyond = device(x + 2, y, z, c), device(x, y, z + 2, c)
    sibling = device(x, y, z, 1 - c)
    greet([*near["X"], *near["Y"], *near["Z"], across, beyond, sibling])
    pending = []

    def index(order, phase, q):
        at = [slice(None)] * 4
        for a in order[:phase]:
            put(at, a, where[a])
        put(at, order[phase], q)
        return tuple(at)

    def key(t, phase, k):
        return (t * 3 + phase) * 6 + k

    def ship(src, dst, to, t, phase, k):
        cp = remote(src, dst, send_sem.at[key(t, phase, k)], recv_sem.at[key(t, phase, k)], to)
        cp.start()
        pending.append(cp)

    def arrived(dst, t, phase, k):
        remote(dst, dst, send_sem.at[key(t, phase, k)], recv_sem.at[key(t, phase, k)], sibling).wait_recv()

    def cols(view, h, t):
        at, size = halves(held[t].shape[-1])[h]
        lead = len(view.shape) - 1
        return view.at[(slice(None),) * lead + (pl.ds(at, size),)]

    def part(ref, t, phase, q, h):
        return cols(ref.at[index(ORDERS[t], phase, q)], h, t)

    def buffers(t, phase):
        ra, rb = relay[t][2 * phase : 2 * phase + 2]
        tl, tr = takes[t][2 * phase : 2 * phase + 2]
        return ra, rb, tl, tr

    def each(dims, body):
        total = 1
        for d in dims:
            total *= d

        def step(i, carry):
            at, rest = [], i
            for d in reversed(dims):
                at.append(rest % d)
                rest = rest // d
            body(tuple(reversed(at)))
            return carry

        if total == 1:
            body(())
        else:
            lax.fori_loop(0, total, step, 0)

    def full(order, phase, q, at):
        idx, k = list(index(order, phase, q)), 0
        for i in range(4):
            if isinstance(idx[i], slice):
                idx[i] = at[k]
                k += 1
        return tuple(idx)

    def begin(t, phase, first=True, second=True):
        order = ORDERS[t]
        p = where[order[phase]]
        left, right = near[order[phase]]
        ra, rb, tl, tr = buffers(t, phase)
        src = held[t]
        far_q, next_q, last_q = (p + 2) % 4, (p + 1) % 4, (p + 3) % 4
        if first:
            ship(part(src, t, phase, far_q, 0), ra, right, t, phase, 0)
            ship(part(src, t, phase, far_q, 1), rb, left, t, phase, 1)
        if second:
            ship(part(src, t, phase, next_q, 1), cols(tl, 1, t), right, t, phase, 2)
            ship(part(src, t, phase, last_q, 0), cols(tr, 0, t), left, t, phase, 3)

    def middle(t, phase):
        order = ORDERS[t]
        p = where[order[phase]]
        left, right = near[order[phase]]
        ra, rb, tl, tr = buffers(t, phase)
        dims = dims_left(order, phase)
        for h, (box, q, to, dst) in enumerate(((ra, (p + 1) % 4, right, tl), (rb, (p + 3) % 4, left, tr))):
            arrived(box, t, phase, h)
            at0, size = halves(held[t].shape[-1])[h]

            def add(at, box=box, q=q, at0=at0, size=size):
                slab = full(order, phase, q, at) + (slice(None), pl.ds(at0, size))
                held[t][slab] = (held[t][slab].astype(F32) + box[at].astype(F32)).astype(BF)

            each(dims, add)
            ship(part(held[t], t, phase, q, h), cols(dst, h, t), to, t, phase, 4 + h)

    def finish(t, phase):
        order = ORDERS[t]
        p = where[order[phase]]
        ra, rb, tl, tr = buffers(t, phase)
        dims = dims_left(order, phase)
        if t < 3 and phase == 0:
            for cp in taken[3 * t : 3 * t + 3]:
                cp.wait()
        else:
            arrived(cols(tl, 1, t), t, phase, 2)
            arrived(cols(tr, 0, t), t, phase, 3)
            arrived(cols(tl, 0, t), t, phase, 4)
            arrived(cols(tr, 1, t), t, phase, 5)

        def add(at):
            slab = full(order, phase, p, at)
            held[t][slab] = (held[t][slab].astype(F32) + tl[at].astype(F32) + tr[at].astype(F32)).astype(BF)

        each(dims, add)

    def fill(t, step):
        axis = ORDERS[t][0]
        at = [slice(None)] * 4
        put(at, axis, (where[axis] + step) % 4)
        at = tuple(at)
        lead = dims_left(ORDERS[t], 0)

        def block(left, right, start, cols_n, put_at):
            rows = flat(left[at])

            value = mul(rows, right[:, pl.ds(pl.multiple_of(start, 128), cols_n)]).astype(BF)
            held[t][at + (slice(None), pl.ds(put_at, cols_n))] = value.reshape(lead + (16, cols_n))

        i = t % 3
        left, right = (mid_t, mid_t, cot_t)[i], (gg, gu, hidden)[i]
        block(left, right, EARLY, ff - EARLY, 0)
        block(in_t, gproj, i * half, half, ff - EARLY)
        if i:
            block(gated_t, gmix, c * half + (i - 1) * quarter, quarter, ff - EARLY + half)

    for cp in loads[:5]:
        cp.wait()
    tall = jnp.concatenate([small[...], jnp.zeros((120, width), F32)], axis=0)
    held[3][:, :, :, :, :, pl.ds(ff - EARLY + half, 128)] = tall.T.astype(BF).reshape(2, 4, 2, 4, 16, 128)
    fill(3, 2)
    begin(3, 0, second=False)
    for cp in loads[5:]:
        cp.wait()
    turn(gated, gated_t)
    for t in (4, 5):
        fill(t, 2)
        begin(t, 0, second=False)
    for t in (0, 1, 2):
        finish(t, 0)
        begin(t, 1)
    for t in (3, 4, 5):
        fill(t, 1)
        fill(t, 3)
        begin(t, 0, first=False)
    for t in (0, 1, 2):
        middle(t, 1)
    for t in (3, 4, 5):
        middle(t, 0)
    for t in (3, 4, 5):
        fill(t, 0)
    for t in (3, 4, 5):
        finish(t, 0)
        begin(t, 1)
    for t in (0, 1, 2):
        finish(t, 1)
        begin(t, 2)
    for t in (3, 4, 5):
        middle(t, 1)
    for t in (0, 1, 2):
        middle(t, 2)
    for t in (3, 4, 5):
        finish(t, 1)
        begin(t, 2)
    for t in (0, 1, 2):
        finish(t, 2)
    late = ff - EARLY
    pieces = []
    for t in range(n):
        wide = (o_gate, o_up, o_down)[t % 3]
        if t < 3:
            pieces.append([(0, EARLY, wide, 0, ff)])
        else:
            i = t - 3
            pieces.append([(0, late, wide, EARLY, ff), (late, half, o_in, i * width, half)])
            if i:
                pieces[-1].append((late + half, quarter, o_out, (i - 1) * quarter, half))
            else:
                pieces[-1].append((late + half, 128, o_small, 0, 128))
    base = [sum(len(p) for p in pieces[:t]) for t in range(n)]

    def spot(out, row, count, col, size):
        return out.at[pl.ds(pl.multiple_of(row, 16), count), pl.ds(pl.multiple_of(col, 128), size)]

    def landing(t, k, dx, dz):
        at, size, out, col, stride = pieces[t][k]
        slot = (xh + dx) % 2 * 4 + (z + dz + 4) % 4
        return spot(out, slot * 16, 16, col + c * stride, size)

    def pass_on(t, k, i, src, dst, to):
        key_ = (base[t] + k) * 7 + i
        cp = remote(src, dst, spread_send.at[key_], spread_recv.at[key_], to)
        cp.start()
        pending.append(cp)

    def landed(t, k, i, dx, dz):
        key_ = (base[t] + k) * 7 + i
        dst = landing(t, k, dx, dz)
        remote(dst, dst, spread_send.at[key_], spread_recv.at[key_], sibling).wait_recv()

    zm, zp = near["Z"]
    keeps = {}

    def spread(t):
        for k, (at, size, out, col, stride) in enumerate(pieces[t]):
            piece = held[t].at[xl, y, xh, z, :, pl.ds(at, size)]
            dst = landing(t, k, 0, 0)
            for i, to in enumerate((across, beyond, zp, zm)):
                pass_on(t, k, i, piece, dst, to)
            keeps[t, k] = pltpu.make_async_copy(piece, dst, local_sem.at[base[t] + k])
            keeps[t, k].start()

    def spread_more(t):
        for k in range(len(pieces[t])):
            landed(t, k, 0, 1, 0)
            mine = landing(t, k, 1, 0)
            pass_on(t, k, 4, mine, mine, zp)
            pass_on(t, k, 5, mine, mine, zm)
            landed(t, k, 1, 0, 2)
            mine = landing(t, k, 0, 2)
            pass_on(t, k, 6, mine, mine, across)

    def share(t):
        for k, (at, size, out, col, stride) in enumerate(pieces[t]):
            keeps[t, k].wait()
            landed(t, k, 2, 0, -1)
            landed(t, k, 3, 0, 1)
            landed(t, k, 4, 1, -1)
            landed(t, k, 5, 1, 1)
            landed(t, k, 6, 1, 2)
            whole = spot(out, 0, 128, col + c * stride, size)
            cp = remote(whole, whole, core_send.at[base[t] + k], core_recv.at[base[t] + k], sibling)
            cp.start()
            pending.append(cp)

    for t in (0, 1, 2):
        spread(t)
    for t in (3, 4, 5):
        middle(t, 2)
    for t in (3, 4, 5):
        finish(t, 2)
        spread(t)
    for step in (spread_more, share):
        for t in range(n):
            step(t)
    for t in range(n):
        for k, (at, size, out, col, stride) in enumerate(pieces[t]):
            dst = spot(out, 0, 128, col + (1 - c) * stride, size)
            remote(dst, dst, core_send.at[base[t] + k], core_recv.at[base[t] + k], sibling).wait_recv()
    for cp in pending:
        cp.wait_send()


def reduce_grads(mid_t, gg, in_t, gproj, small, gu, gated, gmix, cot_t, hidden, *begun):
    n = COUNT
    ins = (mid_t, gg, in_t, gproj, small, gu, gated, gmix, cot_t, hidden)
    width, ff, two = gated.shape[1], gg.shape[1], gated.shape[0]
    half = width // 2
    late = ff - EARLY + half
    widths = (EARLY,) * 3 + (late + 128, late + half // 2, late + half // 2)
    lead = (2, 4, 2, 4, 16)
    held = [pltpu.VMEM(lead + (w,), BF) for w in widths]
    relay, takes = [], []
    for t in range(n):
        for phase in range(3):
            dims = dims_left(ORDERS[t], phase)
            for h in (0, 1):
                relay.append(pltpu.VMEM(dims + (16, halves(widths[t])[h][1]), BF))
                takes.append(pltpu.VMEM(dims + (16, widths[t]), BF))
    bufs = [pltpu.VMEM(a.shape, a.dtype) for a in ins]
    turned = [pltpu.VMEM(lead + (two,), BF)]
    dma = pltpu.SemaphoreType.DMA
    hbm = pl.BlockSpec(memory_space=pltpu.HBM)
    rows = 128
    outs = (2 * ff, 2 * ff, 2 * ff, 3 * width, width, 256)
    return pl.pallas_call(
        reduce_kernel,
        out_shape=tuple(jax.ShapeDtypeStruct((rows, w), BF) for w in outs),
        in_specs=[hbm] * len(ins + begun),
        out_specs=(hbm,) * len(outs),
        scratch_shapes=held + relay + takes + bufs + turned
        + [dma((19,)), dma((108,)), dma((108,)), dma((84,)), dma((84,)), dma((12,)), dma((12,))],
        compiler_params=pltpu.CompilerParams(collective_id=2, has_side_effects=True, vmem_limit_bytes=62 << 20),
    )(*ins, *begun)


def local(tokens, norm_in, w_in, conv_w, w_out, norm_mid, w_gate, w_up, w_down, cotangent):
    gains = jnp.stack([norm_in, norm_mid])
    (
        result, grad_tokens, in_t, mid_t, hidden, gg, gu, gproj, gated, gmix, cot_t, small, *begun
    ) = block_call(tokens[0], cotangent[0], w_in, w_out, w_gate, w_up, w_down, gains, conv_w.T)
    sums = reduce_grads(mid_t, gg, in_t, gproj, small, gu, gated, gmix, cot_t, hidden, *begun)
    g_gate, g_up, g_down, g_in, g_out, g_small = (s.astype(F32) for s in sums)
    g_small = g_small[:, :128] + g_small[:, 128:]
    return (
        result[None],
        grad_tokens[None],
        g_small[:, 0],
        g_in,
        g_small[:, 2:5],
        g_out,
        g_small[:, 1],
        g_gate,
        g_up,
        g_down,
    )


def solution(mesh):
    row, act, vec = P("shard", None), P("replica", "shard", None), P("shard")
    in_specs = (act, vec, row, row, row, vec, row, row, row, act)
    out_specs = (act, act, vec, row, row, row, vec, row, row, row)
    return jax.shard_map(local, mesh=mesh, in_specs=in_specs, out_specs=out_specs, check_vma=False)
```

```python
import jax
import jax.numpy as jnp
from jax import lax
from jax.sharding import PartitionSpec as P
from jax.experimental import pallas as pl
from jax.experimental.pallas import tpu as pltpu

MESH = pl.DeviceIdType.MESH
BF = jnp.bfloat16
F32 = jnp.float32
EPS = 1e-05


def place():
    s = lax.axis_index("shard")
    r = lax.axis_index("replica")
    xl, y = s // 4, s % 4
    z, xh, c = r // 4, (r // 2) % 2, r % 2
    return xl, xh, y, z, c


def device(x, y, z, c):
    x, y, z = (x + 4) % 4, (y + 4) % 4, (z + 4) % 4
    return ((x % 2) * 4 + y, z * 4 + (x // 2) * 2 + c)


def remote(src, dst, send, recv, to):
    return pltpu.make_async_remote_copy(
        src_ref=src, dst_ref=dst, send_sem=send, recv_sem=recv, device_id=to, device_id_type=MESH
    )


def greet(devices):
    barrier = pltpu.get_barrier_semaphore()
    for to in devices:
        pl.semaphore_signal(barrier, inc=1, device_id=to, device_id_type=MESH)
    pl.semaphore_wait(barrier, len(devices))


def mul(left, right):
    return lax.dot_general(left, right, (((1,), (0,)), ((), ())), preferred_element_type=F32)


def times_rows(left, right):
    return lax.dot_general(left, right, (((1,), (1,)), ((), ())), preferred_element_type=F32)


def normalize(values):
    scale = lax.rsqrt(jnp.mean(values * values, axis=-1, keepdims=True) + EPS)
    return values * scale, scale


def norm_back(grad_normed, normed, scale):
    return scale * (grad_normed - normed * jnp.mean(grad_normed * normed, axis=-1, keepdims=True))


def loop(count, body):
    def step(i, carry):
        body(i)
        return carry

    lax.fori_loop(0, count, step, 0)


def chunk(i, size):
    return pl.ds(pl.multiple_of(i * size, size), size)


def flat(value):
    return value.reshape(-1, value.shape[-1])


ORDERS = ("XYZ", "YZX", "ZXY") * 2
SIZES = {"X": (1, 4, 1, 4), "Y": (2, 1, 2, 4), "Z": (2, 4, 2, 1)}


def dims_left(order, phase):
    sizes = [2, 4, 2, 4]
    for axis in order[: phase + 1]:
        for i in {"X": (0, 2), "Y": (1,), "Z": (3,)}[axis]:
            sizes[i] = 1
    return tuple(n for n in sizes if n > 1)


def halves(columns):
    first = columns // 256 * 128
    return (0, first), (first, columns - first)


EARLY = 2048
WIDE = 1024
LEAD = (2, 4, 2, 4, 16)


def put(at, axis, q):
    if axis == "X":
        at[0], at[2] = q % 2, q // 2
    else:
        at[1 if axis == "Y" else 3] = q


def quarter_at(axis, q):
    at = [slice(None)] * 4
    put(at, axis, q)
    return tuple(at)


def turn(source, target):
    size = 128

    def one(i):
        target[:, :, :, :, :, chunk(i, size)] = source[chunk(i, size)].T.reshape(LEAD + (size,))

    loop(source.shape[0] // size, one)


SWAPS = ("tokens", "cot", "gated0", "gated1", "mix", "act", "gam", "gmix", "fore", "back")
TILE = 256


def block_kernel(
    tokens, cot, w_in, w_out, w_gate, w_up, w_down, gains, taps_in,
    o_win, o_wd, o_resid, o_grad_resid, o_vecs,
    o_in_t, o_mid_t, o_hidden, o_gg, o_gu, o_proj, o_gated, o_mix, o_cot_t, o_small, *rest,
):
    begun, rest = [rest[7 * t : 7 * t + 7] for t in range(3)], rest[21:]
    (
        win, wout, wgu, wd, ext, tok2, cot2, act_in, proj, mixed, conv, gated, part, box_mix, box_gam,
    resid, normed, act_mid, hidden, held, gg, gu, gmix, gconv, gproj, vecs, small, scale_mid, mid_t, cot_t,
    local_sem, send_sem, recv_sem, core_send, core_recv, out_sem, early_send, early_recv,
    ) = rest
    xl, xh, y, z, c = place()
    x = xh * 2 + xl
    shard, replica = lax.axis_index("shard"), lax.axis_index("replica")
    own = xl * 4 + y
    length, width = tokens.shape
    half = width // 2
    ff = wd.shape[2]
    rows = wd.shape[1]
    mine = z % 2
    xp, xm = device(x + 1, y, z, c), device(x - 1, y, z, c)
    yp, ym = device(x, y + 1, z, c), device(x, y - 1, z, c)
    zp, zm = device(x, y, z + 1, c), device(x, y, z - 1, c)
    sibling = device(x, y, z, 1 - c)
    nxt, prv = ((shard + 1) % 8, replica), ((shard + 7) % 8, replica)
    first, last = shard == 0, shard == 7

    ext[own] = jnp.concatenate([gains[...].astype(F32), taps_in[...].astype(F32), jnp.zeros((27, 128), F32)], axis=0).astype(BF)
    copies = []
    for i in range(3):
        copies.append((w_in.at[:, pl.ds(pl.multiple_of(i * width + c * half, 128), half)], win.at[own, :, pl.ds(i * half, half)]))
    copies.append((w_gate.at[:, pl.ds(pl.multiple_of(c * ff, 128), ff)], wgu.at[0, own]))
    copies.append((w_up.at[:, pl.ds(pl.multiple_of(c * ff, 128), ff)], wgu.at[1, own]))
    copies.append((w_out, wout.at[own]))
    copies.append((w_down.at[:, pl.ds(pl.multiple_of(c * ff, 128), ff)], wd.at[own]))
    copies.append((tokens, tok2.at[pl.ds(0, length)]))
    copies.append((cot, cot2.at[pl.ds(0, length)]))
    loads = [pltpu.make_async_copy(a, b, local_sem.at[i]) for i, (a, b) in enumerate(copies)]
    for cp in loads:
        cp.start()
    greet([xp, xm, yp, ym, zp, zm, sibling, nxt, prv])

    pending, stores, used = [], [], []

    def store(src, dst):
        stores.append(pltpu.make_async_copy(src, dst, out_sem.at[len(used)]))
        used.append(dst)
        stores[-1].start()

    ending = []

    def fire(cp):
        if ending:
            cp.wait_send()
        else:
            cp.start()
            pending.append(cp.wait_send)

    owner = c == xl

    def only(condition, *bodies):
        before = len(pending)

        @pl.when(condition)
        def _():
            for body in bodies:
                body(WOUT)

        del pending[before:]

    def swap(name, src, dst, to=None):
        k = SWAPS.index(name)
        return remote(src, dst, core_send.at[k], core_recv.at[k], sibling if to is None else to)

    def wd_part(g, u):
        return wd.at[u, pl.ds(pl.multiple_of(g * (rows // 4), rows // 4), rows // 4)]

    parts = [
        (lambda g, u: ext.at[u], False),
        (lambda g, u: win.at[u], False),
        (lambda g, u: wgu.at[g, u], True),
        (lambda g, u: wout.at[u], False),
        (wd_part, True),
        (lambda g, u: wd.at[u, pl.ds(rows // 2, rows // 2)], False),
    ]
    keys, count = {}, 0
    for p in range(len(parts)):
        names = ["y+", "y-", "f+", "f-"]
        for dy in (0, -1, 1, 2):
            for h in (0, 1):
                names.append(("x", dy, h))
                if parts[p][1]:
                    names.append(("z", 1, dy, h))
                    if dy:
                        names.append(("z", 0, dy, h))
        for name in names:
            keys[p, name] = count
            count += 1
    assert count == COPIES

    def send(view, to, k):
        fire(remote(view, view, send_sem.at[k], recv_sem.at[k], to))

    def got(view, k):
        if ending:
            return
        remote(view, view, send_sem.at[k], recv_sem.at[k], yp).wait_recv()

    def cut(view, h):
        hr = view.shape[0] // 2
        return view.at[pl.ds(h * hr, hr)]

    def at_y(dy):
        return xl * 4 + (y + dy + 4) % 4

    def over(dy):
        return (1 - xl) * 4 + (y + dy + 4) % 4

    def send_x(p, dy, h):
        send(cut(parts[p][0](mine, at_y(dy)), h), (xp, xm)[h], keys[p, ("x", dy, h)])

    def send_z(p, other, dy, h):
        if parts[p][1]:
            u = over(dy) if other else at_y(dy)
            send(cut(parts[p][0](mine, u), h), (zp, zm)[h], keys[p, ("z", other, dy, h)])

    def launch_y(p):
        view = parts[p][0]
        send(view(mine, own), yp, keys[p, "y+"])
        send(view(mine, own), ym, keys[p, "y-"])

    def launch_x(p):
        for h in (0, 1):
            send_x(p, 0, h)

    def stage_a(p):
        view = parts[p][0]
        got(view(mine, at_y(-1)), keys[p, "y+"])
        send(cut(view(mine, at_y(-1)), 0), yp, keys[p, "f+"])
        for h in (0, 1):
            send_z(p, 0, -1, h)
            send_x(p, -1, h)
        got(view(mine, at_y(1)), keys[p, "y-"])
        send(cut(view(mine, at_y(1)), 1), ym, keys[p, "f-"])
        for h in (0, 1):
            send_z(p, 0, 1, h)
            send_x(p, 1, h)

    def stage_b(p):
        view = parts[p][0]
        for h in (0, 1):
            got(cut(view(mine, at_y(2)), h), keys[p, ("f+", "f-")[h]])
            send_z(p, 0, 2, h)
            send_x(p, 2, h)

    def stage_c(p, *dys):
        view = parts[p][0]
        for dy in dys or (0, -1, 1, 2):
            for h in (0, 1):
                got(cut(view(mine, over(dy)), h), keys[p, ("x", dy, h)])
                send_z(p, 1, dy, h)

    def stage_d(p):
        view = parts[p][0]
        for h in (0, 1):
            for dy in (0, -1, 1, 2):
                if dy:
                    got(cut(view(1 - mine, at_y(dy)), h), keys[p, ("z", 0, dy, h)])
                got(cut(view(1 - mine, over(dy)), h), keys[p, ("z", 1, dy, h)])

    EXT, WIN, WGU, WOUT, WDZ, WDX = range(6)
    lower, upper = pl.ds(0, length), pl.ds(length, length)
    launch_y(EXT)
    launch_x(EXT)
    for cp in loads[3:5]:
        cp.wait()
    launch_y(WGU)
    launch_x(WGU)
    for cp in loads[:3]:
        cp.wait()
    launch_y(WIN)
    launch_x(WIN)
    for cp in loads[7:]:
        cp.wait()
    fire(swap("tokens", tok2.at[lower], tok2.at[upper]))
    fire(swap("cot", cot2.at[lower], cot2.at[upper]))
    for cp in loads[5:7]:
        cp.wait()
    only(owner, launch_x)
    launch_x(WDZ)
    launch_x(WDX)
    for stage in (stage_a, stage_b, stage_c):
        stage(EXT)
    for u in range(8):
        vecs[:, pl.ds(u * 128, 128)] = ext[u, pl.ds(0, 16)].astype(F32)
    small[...] = jnp.zeros_like(small)
    mixed[:, pl.ds(0, 8)] = jnp.zeros((2, 8, half), F32)
    gconv[:, pl.ds(length, 8)] = jnp.zeros((2, 8, half), F32)
    swap("tokens", tok2.at[lower], tok2.at[upper]).wait_recv()
    rc = 32

    def norm_in_step(i):
        v, _ = normalize(tok2[chunk(i, rc)].astype(F32))
        act_in[chunk(i, rc)] = (v * vecs[0:1]).astype(BF)

    loop(2 * length // rc, norm_in_step)
    turn(act_in, mid_t)
    store(mid_t, o_in_t)
    in_store = stores.pop()
    stage_c(WGU, 0)
    stage_a(WGU)
    only(owner, launch_y)
    stage_a(WIN)
    launch_y(WDZ)
    stage_c(WGU, -1, 1)
    stage_b(WGU)
    only(owner, stage_a)
    launch_y(WDX)
    stage_b(WIN)
    stage_c(WGU, 2)
    stage_a(WDZ)
    swap("cot", cot2.at[lower], cot2.at[upper]).wait_recv()
    turn(cot2, cot_t)
    store(cot_t, o_cot_t)
    stage_c(WIN)

    def proj_step(j):
        proj[:, chunk(j, TILE)] = mul(act_in[...], flat(win[:, :, chunk(j, TILE)]))

    store(win, o_win)
    store(vecs, o_vecs)
    loop(3 * half // TILE, proj_step)

    def b_of(at):
        return proj[at, pl.ds(0, half)]

    def c_of(at):
        return proj[at, pl.ds(half, half)]

    def x_of(at):
        return proj[at, pl.ds(2 * half, half)]

    def mixed_step(i):
        for q in (0, 1):
            at = pl.ds(pl.multiple_of(q * length + i * rc, rc), rc)
            mixed[q, pl.ds(pl.multiple_of(8 + i * rc, 8), rc)] = (b_of(at) * x_of(at)).astype(BF).astype(F32)

    loop(length // rc, mixed_step)
    fore = swap("fore", mixed.at[:, pl.ds(length, 8)], mixed.at[:, pl.ds(0, 8)], nxt)
    back = swap("back", gconv.at[:, pl.ds(0, 8)], gconv.at[:, pl.ds(length, 8)], prv)

    @pl.when(jnp.logical_not(last))
    def _():
        fore.start()

    only(owner, stage_b)
    stage_c(WDZ, 0)
    stage_a(WDX)

    @pl.when(jnp.logical_not(first))
    def _():
        fore.wait_recv()

    taps = [vecs[pl.ds(2 + k, 1), pl.ds(pl.multiple_of(c * half, 128), half)] for k in range(3)]
    rq = 64

    def conv_step(i):
        for q in (0, 1):
            window = mixed[q, pl.ds(pl.multiple_of(i * rq, 8), rq + 8)]
            value = taps[0] * window[6 : 6 + rq] + taps[1] * window[7 : 7 + rq] + taps[2] * window[8 : 8 + rq]
            at = pl.ds(pl.multiple_of(q * length + i * rq, rq), rq)
            conv[at] = value
            gated[at, pl.ds(pl.multiple_of(c * half, 128), half)] = (c_of(at) * value).astype(BF)

    loop(length // rq, conv_step)
    gated_mine = gated.at[:, pl.ds(pl.multiple_of(c * half, 128), half)]
    gated_other = gated.at[:, pl.ds(pl.multiple_of((1 - c) * half, 128), half)]
    fire(swap("gated0", gated_mine.at[lower], gated_mine.at[upper]))
    fire(swap("gated1", gated_mine.at[upper], gated_mine.at[lower]))
    stage_b(WDZ)
    stage_c(WDZ, -1, 1)
    only(jnp.logical_not(owner), stage_c)
    wout_mine = wout.at[pl.ds(pl.multiple_of(c * 4, 4), 4)]

    def mix_step(j):
        part[:, chunk(j, TILE)] = mul(gated_mine[...], flat(wout_mine[:, :, chunk(j, TILE)]))

    loop(width // TILE, mix_step)
    mix_swap = swap("mix", part.at[upper], box_mix)
    mix_swap.start()
    stage_b(WDX)
    mix_swap.wait_recv()

    def norm_mid_step(i):
        at = chunk(i, rc)
        v = tok2[at].astype(F32) + part[at] + box_mix[at]
        n, s = normalize(v)
        resid[at] = v
        normed[at] = n
        scale_mid[at] = jnp.broadcast_to(s, (rc, 128))
        act_mid[at] = (n * vecs[1:2]).astype(BF)

    loop(length // rc, norm_mid_step)
    store(resid, o_resid)
    act_swap = swap("act", act_mid.at[lower], act_mid.at[upper])
    act_swap.start()
    stage_c(WDZ, 2)
    act_swap.wait_recv()
    in_store.wait()
    turn(act_mid, mid_t)
    store(mid_t, o_mid_t)
    stage_d(WGU)

    where = {"X": x, "Y": y, "Z": z}
    near = {"X": (xm, xp), "Y": (ym, yp), "Z": (zm, zp)}
    eh = EARLY // 2

    def early_at(t, step):
        axis = ORDERS[t][0]
        return quarter_at(axis, (where[axis] + step) % 4)

    def early_fill(t, step):
        at = early_at(t, step)
        lead = dims_left(ORDERS[t], 0) + (16, WIDE)
        tall, right = flat((mid_t, mid_t, cot_t)[t][at]), (gg, gu, hidden)[t]

        def one(j):
            value = mul(tall, right[:, chunk(j, WIDE)]).astype(BF)
            held[(t,) + at + (slice(None), chunk(j, WIDE))] = value.reshape(lead)

        loop(EARLY // WIDE, one)

    def early_cols(view, h):
        return view.at[(slice(None),) * (len(view.shape) - 1) + (pl.ds(h * eh, eh),)]

    def keep(t):
        store(held.at[(t,) + early_at(t, 0)], begun[t][0])
        store(early_cols(held.at[(t,) + early_at(t, 1)], 0), begun[t][1])
        store(early_cols(held.at[(t,) + early_at(t, 3)], 1), begun[t][2])

    def early_copy(t, k):
        to_right = k in (0, 2)
        h = (0, 1, 1, 0)[k]
        step = 2 if k < 2 else (1 if to_right else 3)
        src = early_cols(held.at[(t,) + early_at(t, step)], h)
        dst = begun[t][3 + k]
        to = near[ORDERS[t][0]][1 if to_right else 0]
        return remote(src, dst, early_send.at[t * 4 + k], early_recv.at[t * 4 + k], to)

    def gate_step(j):
        at = chunk(j, TILE)
        gate = mul(act_mid[...], flat(wgu[0, :, :, at]))
        up = mul(act_mid[...], flat(wgu[1, :, :, at]))
        sig = jax.nn.sigmoid(gate)
        silu = gate * sig
        hidden[:, at] = (silu * up).astype(BF)
        factor = up * (sig * (1.0 + gate * (1.0 - sig)))
        spot = (slice(None),) * 4 + (chunk(j % (EARLY // TILE), TILE),)
        held[(j // (EARLY // TILE), 0) + spot] = factor.astype(BF).reshape(LEAD[1:] + (TILE,))
        held[(j // (EARLY // TILE), 1) + spot] = silu.astype(BF).reshape(LEAD[1:] + (TILE,))

    loop(ff // TILE, gate_step)
    store(hidden, o_hidden)
    early_fill(2, 2)
    fire(early_copy(2, 0))
    fire(early_copy(2, 1))
    early_fill(2, 1)
    fire(early_copy(2, 2))
    early_fill(2, 3)
    fire(early_copy(2, 3))
    early_fill(2, 0)
    keep(2)
    stage_c(WDX)
    stage_d(WDZ)

    def grad_hidden_step(j):
        at = chunk(j, TILE)
        g = mul(cot2[...], flat(wd[:, :, at]))
        spot = (slice(None),) * 4 + (chunk(j % (EARLY // TILE), TILE),)
        gg[:, at] = (g * flat(held[(j // (EARLY // TILE), 0) + spot]).astype(F32)).astype(BF)
        gu[:, at] = (g * flat(held[(j // (EARLY // TILE), 1) + spot]).astype(F32)).astype(BF)

    loop(ff // TILE, grad_hidden_step)
    store(gg.at[:, pl.ds(EARLY, ff - EARLY)], o_gg)
    store(gu.at[:, pl.ds(EARLY, ff - EARLY)], o_gu)
    store(wd, o_wd)
    for t in (0, 1):
        early_fill(t, 2)
        fire(early_copy(t, 0))
        fire(early_copy(t, 1))
    for t in (0, 1):
        early_fill(t, 1)
        fire(early_copy(t, 2))
    swap("mix", part.at[upper], box_mix).wait_send()

    def gam_step(j):
        u = pl.ds(j * 2, 2)
        part[:, chunk(j, TILE)] = times_rows(gg[...], flat(wgu[0, u])) + times_rows(gu[...], flat(wgu[1, u]))

    loop(4, gam_step)
    gam_swap = swap("gam", part.at[upper], box_gam)
    gam_swap.start()
    for t in (0, 1):
        early_fill(t, 3)
        fire(early_copy(t, 3))
    gam_swap.wait_recv()

    def resid_step(i):
        at = chunk(i, rc)
        g = part[at] + box_gam[at]
        n = normed[at]
        small[1:2] = small[1:2] + jnp.sum(g * n, axis=0, keepdims=True)
        full = cot2[at].astype(F32) + norm_back(g * vecs[1:2], n, scale_mid[at, 0:1])
        box_gam[at] = full
        gmix[at] = full.astype(BF)

    loop(length // rc, resid_step)
    gmix_swap = swap("gmix", gmix.at[lower], gmix.at[upper])
    gmix_swap.start()
    for t in (0, 1):
        early_fill(t, 0)
        keep(t)
    gam_swap.wait_send()

    def ffn_step(j):
        u = pl.ds(j * 2, 2)
        part[:, chunk(j, TILE)] = times_rows(hidden[...], flat(wd[u]))

    loop(4, ffn_step)
    store(box_gam, o_grad_resid)
    gmix_swap.wait_recv()
    for q in (0, 1):
        box_mix[:, pl.ds(q * half, half)] = times_rows(gmix[pl.ds(q * length, length)], flat(wout_mine[...]))

    def gconv_step(i):
        for q in (0, 1):
            at = pl.ds(pl.multiple_of(q * length + i * rc, rc), rc)
            window = mixed[q, pl.ds(pl.multiple_of(i * rc, 8), rc + 8)]
            g = box_mix[pl.ds(pl.multiple_of(i * rc, rc), rc), pl.ds(q * half, half)]
            gc = g * c_of(at)
            gconv[q, pl.ds(pl.multiple_of(i * rc, 8), rc)] = gc
            gproj[at, pl.ds(half, half)] = (g * conv[at]).astype(BF)
            for k in range(3):
                spot = (pl.ds(2 + k, 1), pl.ds(pl.multiple_of(c * half, 128), half))
                small[spot] = small[spot] + jnp.sum(gc * window[6 + k : 6 + k + rc], axis=0, keepdims=True)

    loop(length // rc, gconv_step)

    @pl.when(jnp.logical_not(first))
    def _():
        back.start()

    @pl.when(jnp.logical_not(last))
    def _():
        back.wait_recv()

    def gproj_step(i):
        for q in (0, 1):
            at = pl.ds(pl.multiple_of(q * length + i * rc, rc), rc)
            window = gconv[q, pl.ds(pl.multiple_of(i * rc, 8), rc + 8)]
            gm = taps[2] * window[0:rc] + taps[1] * window[1 : rc + 1] + taps[0] * window[2 : rc + 2]
            gproj[at, pl.ds(0, half)] = (gm * x_of(at)).astype(BF)
            gproj[at, pl.ds(2 * half, half)] = (gm * b_of(at)).astype(BF)

    loop(length // rc, gproj_step)
    swap("gated0", gated_other.at[upper], gated_other.at[upper]).wait_recv()
    swap("gated1", gated_other.at[lower], gated_other.at[lower]).wait_recv()
    store(gproj, o_proj)
    store(gated, o_gated)
    store(gmix, o_mix)
    store(small, o_small)
    for t in range(3):
        for k in range(4):
            early_copy(t, k).wait_recv()
    for wait in pending:
        wait()

    ending.append(True)
    only(owner, launch_x, launch_y, stage_a, stage_b)
    act_swap.wait_send()
    gmix_swap.wait_send()

    @pl.when(jnp.logical_not(last))
    def _():
        fore.wait_send()

    @pl.when(jnp.logical_not(first))
    def _():
        back.wait_send()

    for cp in stores:
        cp.wait()


COPIES = 6 * 12 + 2 * 14


def block_call(tokens, cot, w_in, w_out, w_gate, w_up, w_down, gains, taps):
    length, width = tokens.shape
    rows, ff = w_in.shape[0], w_gate.shape[1] // 2
    half = width // 2
    two = 2 * length
    hbm = pl.BlockSpec(memory_space=pltpu.HBM)
    vm = pl.BlockSpec(memory_space=pltpu.VMEM)

    def out(*shape, dtype=BF):
        return jax.ShapeDtypeStruct(shape, dtype)

    def mem(*shape, dtype=BF):
        return pltpu.VMEM(shape, dtype)

    firsts = [dims_left(ORDERS[t], 0) + (16,) for t in range(3)]
    early = [out(*firsts[t], EARLY if k == 0 else EARLY // 2) for t in range(3) for k in range(7)]
    dma = pltpu.SemaphoreType.DMA
    return pl.pallas_call(
        block_kernel,
        out_shape=(
            out(8, rows, 3 * half), out(8, rows, ff), out(length, width, dtype=F32), out(length, width, dtype=F32),
            out(16, width, dtype=F32), out(*LEAD, two), out(*LEAD, two), out(two, ff),
            out(two, ff - EARLY), out(two, ff - EARLY), out(two, 3 * half), out(two, width), out(two, width), out(*LEAD, two),
            out(8, width, dtype=F32), *early,
        ),
        in_specs=[hbm] * 7 + [vm] * 2,
        out_specs=(hbm,) * 36,
        scratch_shapes=[
            mem(8, rows, 3 * half), mem(8, rows, width), mem(2, 8, rows, ff), mem(8, rows, ff), mem(8, 32, 128),
            mem(two, width), mem(two, width), mem(two, width), mem(two, 3 * half, dtype=F32),
            mem(2, length + 8, half, dtype=F32), mem(two, half, dtype=F32), mem(two, width), mem(two, width, dtype=F32),
            mem(length, width, dtype=F32), mem(length, width, dtype=F32), mem(length, width, dtype=F32),
            mem(length, width, dtype=F32), mem(two, width),
            mem(two, ff), mem(3, *LEAD, EARLY), mem(two, ff), mem(two, ff), mem(two, width),
            mem(2, length + 8, half, dtype=F32), mem(two, 3 * half), mem(16, width, dtype=F32), mem(8, width, dtype=F32),
            mem(length, 128, dtype=F32), mem(*LEAD, two), mem(*LEAD, two),
            dma((9,)), dma((COPIES,)), dma((COPIES,)), dma((len(SWAPS),)), dma((len(SWAPS),)), dma((48,)), dma((12,)), dma((12,)),
        ],
        compiler_params=pltpu.CompilerParams(collective_id=1, has_side_effects=True, vmem_limit_bytes=62 << 20),
    )(tokens, cot, w_in, w_out, w_gate, w_up, w_down, gains, taps)
COUNT = 6
INS = 16


def reduce_kernel(*refs):
    n = COUNT
    ins, refs = refs[:INS], refs[INS:]
    begun, refs = refs[:21], refs[21:]
    outs, refs = refs[:8], refs[8:]
    held, refs = refs[:n], refs[n:]
    relay, refs = [refs[6 * t : 6 * t + 6] for t in range(n)], refs[6 * n :]
    takes, refs = [refs[6 * t : 6 * t + 6] for t in range(n)], refs[6 * n :]
    bufs, refs = refs[:INS], refs[INS:]
    turned, refs = refs[:1], refs[1:]
    (sums, box_ffn, box_gai, out_res), refs = refs[:4], refs[4:]
    local_sem, send_sem, recv_sem, spread_send, spread_recv, core_send, core_recv = refs
    o_gate, o_up, o_down, o_in, o_out, o_small, result, grad_tokens = outs
    xl, xh, y, z, c = place()
    x = xh * 2 + xl
    loads = [pltpu.make_async_copy(a, b, local_sem.at[i]) for i, (a, b) in enumerate(zip(ins, bufs))]
    in_t, gproj, cot_t, hidden, gated, gmix, mid_t, gu, win, grad_resid, vecs, tokens, small, gg, wd, resid = bufs
    (gated_t,) = turned
    half = gproj.shape[1] // 3
    ff = hidden.shape[1]
    length = tokens.shape[0]
    width = half * 2
    quarter = half // 2
    where = {"X": x, "Y": y, "Z": z}
    near = {
        "X": (device(x - 1, y, z, c), device(x + 1, y, z, c)),
        "Y": (device(x, y - 1, z, c), device(x, y + 1, z, c)),
        "Z": (device(x, y, z - 1, c), device(x, y, z + 1, c)),
    }
    taken = []
    for t in range(3):
        axis = ORDERS[t][0]
        p, low, high = where[axis], pl.ds(0, EARLY // 2), pl.ds(EARLY // 2, EARLY // 2)
        lead = (slice(None),) * len(dims_left(axis, 0)) + (slice(None),)
        boxes = (
            held[t].at[quarter_at(axis, p)],
            held[t].at[quarter_at(axis, (p + 1) % 4)].at[lead + (low,)],
            held[t].at[quarter_at(axis, (p + 3) % 4)].at[lead + (high,)],
            relay[t][0],
            relay[t][1],
            takes[t][0].at[lead + (high,)],
            takes[t][1].at[lead + (low,)],
        )
        for k in (1, 2, 3, 4, 0, 5, 6):
            i = 7 * t + k
            taken.append(pltpu.make_async_copy(begun[i], boxes[k], local_sem.at[INS + i]))
    firsts = [cp for t in range(3) for cp in taken[7 * t : 7 * t + 4]]
    others = [cp for t in range(3) for cp in taken[7 * t + 4 : 7 * t + 7]]
    for cp in (*firsts, *loads[:8], *others, *loads[8:]):
        cp.start()
    across, beyond = device(x + 2, y, z, c), device(x, y, z + 2, c)
    sibling = device(x, y, z, 1 - c)
    greet([*near["X"], *near["Y"], *near["Z"], across, beyond, sibling])
    pending = []

    def index(order, phase, q):
        at = [slice(None)] * 4
        for a in order[:phase]:
            put(at, a, where[a])
        put(at, order[phase], q)
        return tuple(at)

    def key(t, phase, k):
        return (t * 3 + phase) * 6 + k

    def ship(src, dst, to, t, phase, k):
        cp = remote(src, dst, send_sem.at[key(t, phase, k)], recv_sem.at[key(t, phase, k)], to)
        cp.start()
        pending.append(cp)

    def arrived(dst, t, phase, k):
        remote(dst, dst, send_sem.at[key(t, phase, k)], recv_sem.at[key(t, phase, k)], sibling).wait_recv()

    def cols(view, h, t):
        at, size = halves(held[t].shape[-1])[h]
        lead = len(view.shape) - 1
        return view.at[(slice(None),) * lead + (pl.ds(at, size),)]

    def part(ref, t, phase, q, h):
        return cols(ref.at[index(ORDERS[t], phase, q)], h, t)

    def buffers(t, phase):
        ra, rb = relay[t][2 * phase : 2 * phase + 2]
        tl, tr = takes[t][2 * phase : 2 * phase + 2]
        return ra, rb, tl, tr

    def each(dims, body):
        total = 1
        for d in dims:
            total *= d

        def step(i, carry):
            at, rest = [], i
            for d in reversed(dims):
                at.append(rest % d)
                rest = rest // d
            body(tuple(reversed(at)))
            return carry

        if total == 1:
            body(())
        else:
            lax.fori_loop(0, total, step, 0)

    def full(order, phase, q, at):
        idx, k = list(index(order, phase, q)), 0
        for i in range(4):
            if isinstance(idx[i], slice):
                idx[i] = at[k]
                k += 1
        return tuple(idx)

    def begin(t, phase, first=True, second=True):
        order = ORDERS[t]
        p = where[order[phase]]
        left, right = near[order[phase]]
        ra, rb, tl, tr = buffers(t, phase)
        src = held[t]
        far_q, next_q, last_q = (p + 2) % 4, (p + 1) % 4, (p + 3) % 4
        if first:
            ship(part(src, t, phase, far_q, 0), ra, right, t, phase, 0)
            ship(part(src, t, phase, far_q, 1), rb, left, t, phase, 1)
        if second:
            ship(part(src, t, phase, next_q, 1), cols(tl, 1, t), right, t, phase, 2)
            ship(part(src, t, phase, last_q, 0), cols(tr, 0, t), left, t, phase, 3)

    def middle(t, phase):
        order = ORDERS[t]
        p = where[order[phase]]
        left, right = near[order[phase]]
        ra, rb, tl, tr = buffers(t, phase)
        dims = dims_left(order, phase)
        begun_here = t < 3 and phase == 0
        if begun_here:
            for cp in taken[7 * t : 7 * t + 4]:
                cp.wait()
        for h, (box, q, to, dst) in enumerate(((ra, (p + 1) % 4, right, tl), (rb, (p + 3) % 4, left, tr))):
            if not begun_here:
                arrived(box, t, phase, h)
            at0, size = halves(held[t].shape[-1])[h]

            def add(at, box=box, q=q, at0=at0, size=size):
                slab = full(order, phase, q, at) + (slice(None), pl.ds(at0, size))
                held[t][slab] = (held[t][slab].astype(F32) + box[at].astype(F32)).astype(BF)

            each(dims, add)
            ship(part(held[t], t, phase, q, h), cols(dst, h, t), to, t, phase, 4 + h)

    def finish(t, phase):
        order = ORDERS[t]
        p = where[order[phase]]
        ra, rb, tl, tr = buffers(t, phase)
        dims = dims_left(order, phase)
        if t < 3 and phase == 0:
            for cp in taken[7 * t + 4 : 7 * t + 7]:
                cp.wait()
        else:
            arrived(cols(tl, 1, t), t, phase, 2)
            arrived(cols(tr, 0, t), t, phase, 3)
        arrived(cols(tl, 0, t), t, phase, 4)
        arrived(cols(tr, 1, t), t, phase, 5)

        def add(at):
            slab = full(order, phase, p, at)
            held[t][slab] = (held[t][slab].astype(F32) + tl[at].astype(F32) + tr[at].astype(F32)).astype(BF)

        each(dims, add)

    def fill(t, step):
        axis = ORDERS[t][0]
        at = [slice(None)] * 4
        put(at, axis, (where[axis] + step) % 4)
        at = tuple(at)
        lead = dims_left(ORDERS[t], 0)

        def block(left, right, start, cols_n, put_at):
            rows = flat(left[at])

            value = mul(rows, right[:, pl.ds(pl.multiple_of(start, 128), cols_n)]).astype(BF)
            held[t][at + (slice(None), pl.ds(put_at, cols_n))] = value.reshape(lead + (16, cols_n))

        i = t % 3
        left, right = (mid_t, mid_t, cot_t)[i], (gg, gu, hidden)[i]
        block(left, right, EARLY if i == 2 else 0, ff - EARLY, 0)
        block(in_t, gproj, i * half, half, ff - EARLY)
        if i:
            block(gated_t, gmix, c * half + (i - 1) * quarter, quarter, ff - EARLY + half)

    def swap(k, dst):
        return remote(sums.at[pl.ds(length, length)], dst, core_send.at[12 + k], core_recv.at[12 + k], sibling)

    def gai_step(j):
        sums[:, chunk(j, TILE)] = times_rows(gproj[...], flat(win[pl.ds(j * 2, 2)]))

    def ffn_step(j):
        sums[:, chunk(j, TILE)] = times_rows(hidden[...], flat(wd[pl.ds(j * 2, 2)]))

    def final_step(i):
        at = chunk(i, 32)
        g = sums[at] + box_gai[at]
        normed, scale = normalize(tokens[at].astype(F32))
        small[0:1] = small[0:1] + jnp.sum(g * normed, axis=0, keepdims=True)
        grad_resid[at] = grad_resid[at] + norm_back(g * vecs[0:1], normed, scale)

    def own_ffn_step(i):
        at = chunk(i, 32)
        resid[at] = resid[at] + sums[at]

    def result_step(i):
        at = chunk(i, 32)
        out_res[at] = (resid[at] + box_ffn[at]).astype(BF)

    for t in (0, 1, 2):
        middle(t, 0)
    for cp in loads[:6]:
        cp.wait()
    turn(gated, gated_t)
    fill(5, 2)
    begin(5, 0, second=False)
    for cp in loads[6:9]:
        cp.wait()
    loop(4, gai_step)
    gai_swap = swap(0, box_gai)
    gai_swap.start()
    fill(4, 2)
    begin(4, 0, second=False)
    for t in (5, 4):
        fill(t, 1)
        fill(t, 3)
        begin(t, 0, first=False)
    for cp in loads[9:]:
        cp.wait()
    gai_swap.wait_recv()
    loop(length // 32, final_step)
    back = [pltpu.make_async_copy(grad_resid, grad_tokens, local_sem.at[INS + 21])]
    back[0].start()
    tall = jnp.concatenate([small[...], jnp.zeros((120, width), F32)], axis=0)
    held[3][:, :, :, :, :, pl.ds(ff - EARLY + half, 128)] = tall.T.astype(BF).reshape(2, 4, 2, 4, 16, 128)
    fill(3, 2)
    begin(3, 0, second=False)
    fill(3, 1)
    fill(3, 3)
    begin(3, 0, first=False)
    middle(5, 0)
    middle(4, 0)
    for t in (0, 1, 2):
        finish(t, 0)
        begin(t, 1)
    middle(3, 0)
    for t in (5, 4, 3):
        fill(t, 0)
    for t in (0, 1, 2):
        middle(t, 1)
    gai_swap.wait_send()
    loop(4, ffn_step)
    ffn_swap = swap(1, box_ffn)
    ffn_swap.start()
    loop(length // 32, own_ffn_step)
    for t in (5, 4, 3):
        finish(t, 0)
        begin(t, 1)
    for t in (0, 1, 2):
        finish(t, 1)
        begin(t, 2)
    ffn_swap.wait_recv()
    loop(length // 32, result_step)
    back.append(pltpu.make_async_copy(out_res, result, local_sem.at[INS + 22]))
    back[1].start()
    for t in (3, 4, 5):
        middle(t, 1)
    for t in (0, 1, 2):
        middle(t, 2)
    for t in (3, 4, 5):
        finish(t, 1)
        begin(t, 2)
    for t in (0, 1, 2):
        finish(t, 2)
    late = ff - EARLY
    pieces = []
    for t in range(n):
        wide = (o_gate, o_up, o_down)[t % 3]
        if t < 3:
            pieces.append([(0, EARLY, wide, 0, ff)])
        else:
            i = t - 3
            pieces.append([(0, late, wide, EARLY, ff), (late, half, o_in, i * width, half)])
            if i:
                pieces[-1].append((late + half, quarter, o_out, (i - 1) * quarter, half))
            else:
                pieces[-1].append((late + half, 128, o_small, 0, 128))
    base = [sum(len(p) for p in pieces[:t]) for t in range(n)]

    def spot(out, row, count, col, size):
        return out.at[pl.ds(pl.multiple_of(row, 16), count), pl.ds(pl.multiple_of(col, 128), size)]

    def landing(t, k, dx, dz):
        at, size, out, col, stride = pieces[t][k]
        slot = (xh + dx) % 2 * 4 + (z + dz + 4) % 4
        return spot(out, slot * 16, 16, col + c * stride, size)

    def pass_on(t, k, i, src, dst, to):
        key_ = (base[t] + k) * 7 + i
        cp = remote(src, dst, spread_send.at[key_], spread_recv.at[key_], to)
        cp.start()
        pending.append(cp)

    def landed(t, k, i, dx, dz):
        key_ = (base[t] + k) * 7 + i
        dst = landing(t, k, dx, dz)
        remote(dst, dst, spread_send.at[key_], spread_recv.at[key_], sibling).wait_recv()

    zm, zp = near["Z"]
    keeps = {}

    def spread(t):
        for k, (at, size, out, col, stride) in enumerate(pieces[t]):
            piece = held[t].at[xl, y, xh, z, :, pl.ds(at, size)]
            dst = landing(t, k, 0, 0)
            for i, to in enumerate((across, beyond, zp, zm)):
                pass_on(t, k, i, piece, dst, to)
            keeps[t, k] = pltpu.make_async_copy(piece, dst, local_sem.at[base[t] + k])
            keeps[t, k].start()

    def spread_more(t):
        for k in range(len(pieces[t])):
            landed(t, k, 0, 1, 0)
            mine = landing(t, k, 1, 0)
            pass_on(t, k, 4, mine, mine, zp)
            pass_on(t, k, 5, mine, mine, zm)
            landed(t, k, 1, 0, 2)
            mine = landing(t, k, 0, 2)
            pass_on(t, k, 6, mine, mine, across)

    def share(t):
        for k, (at, size, out, col, stride) in enumerate(pieces[t]):
            keeps[t, k].wait()
            landed(t, k, 2, 0, -1)
            landed(t, k, 3, 0, 1)
            landed(t, k, 4, 1, -1)
            landed(t, k, 5, 1, 1)
            landed(t, k, 6, 1, 2)
            whole = spot(out, 0, 128, col + c * stride, size)
            cp = remote(whole, whole, core_send.at[base[t] + k], core_recv.at[base[t] + k], sibling)
            cp.start()
            pending.append(cp)

    for t in (0, 1, 2):
        spread(t)
    for t in (3, 4, 5):
        middle(t, 2)
    for t in (3, 4, 5):
        finish(t, 2)
        spread(t)
    for step in (spread_more, share):
        for t in range(n):
            step(t)
    for t in range(n):
        for k, (at, size, out, col, stride) in enumerate(pieces[t]):
            dst = spot(out, 0, 128, col + (1 - c) * stride, size)
            remote(dst, dst, core_send.at[base[t] + k], core_recv.at[base[t] + k], sibling).wait_recv()
    for cp in back:
        cp.wait()
    ffn_swap.wait_send()
    for cp in pending:
        cp.wait_send()


def reduce_grads(tokens, win, wd, resid, grad_resid, vecs, in_t, mid_t, hidden, gg, gu, gproj, gated, gmix, cot_t, small, *begun):
    n = COUNT
    ins = (in_t, gproj, cot_t, hidden, gated, gmix, mid_t, gu, win, grad_resid, vecs, tokens, small, gg, wd, resid)
    width, ff, two = gated.shape[1], hidden.shape[1], gated.shape[0]
    length = two // 2
    half = width // 2
    late = ff - EARLY + half
    widths = (EARLY,) * 3 + (late + 128, late + half // 2, late + half // 2)
    lead = (2, 4, 2, 4, 16)
    held = [pltpu.VMEM(lead + (w,), BF) for w in widths]
    relay, takes = [], []
    for t in range(n):
        for phase in range(3):
            dims = dims_left(ORDERS[t], phase)
            for h in (0, 1):
                relay.append(pltpu.VMEM(dims + (16, halves(widths[t])[h][1]), BF))
                takes.append(pltpu.VMEM(dims + (16, widths[t]), BF))
    bufs = [pltpu.VMEM(a.shape, a.dtype) for a in ins]
    turned = [pltpu.VMEM(lead + (two,), BF)]
    one = pltpu.VMEM((length, width), F32)
    own = [pltpu.VMEM((two, width), F32), one, one, pltpu.VMEM((length, width), BF)]
    dma = pltpu.SemaphoreType.DMA
    hbm = pl.BlockSpec(memory_space=pltpu.HBM)
    rows = 128
    outs = (2 * ff, 2 * ff, 2 * ff, 3 * width, width, 256)
    return pl.pallas_call(
        reduce_kernel,
        out_shape=tuple(jax.ShapeDtypeStruct((rows, w), BF) for w in outs)
        + (jax.ShapeDtypeStruct((length, width), BF), jax.ShapeDtypeStruct((length, width), F32)),
        in_specs=[hbm] * len(ins + begun),
        out_specs=(hbm,) * 8,
        scratch_shapes=held + relay + takes + bufs + turned + own
        + [dma((39,)), dma((108,)), dma((108,)), dma((84,)), dma((84,)), dma((14,)), dma((14,))],
        compiler_params=pltpu.CompilerParams(collective_id=2, has_side_effects=True, vmem_limit_bytes=62 << 20),
    )(*ins, *begun)


def local(tokens, norm_in, w_in, conv_w, w_out, norm_mid, w_gate, w_up, w_down, cotangent):
    gains = jnp.stack([norm_in, norm_mid])
    kept = block_call(tokens[0], cotangent[0], w_in, w_out, w_gate, w_up, w_down, gains, conv_w.T)
    *sums, result, grad_tokens = reduce_grads(tokens[0], *kept)
    g_gate, g_up, g_down, g_in, g_out, g_small = (s.astype(F32) for s in sums)
    g_small = g_small[:, :128] + g_small[:, 128:]
    return (
        result[None],
        grad_tokens[None],
        g_small[:, 0],
        g_in,
        g_small[:, 2:5],
        g_out,
        g_small[:, 1],
        g_gate,
        g_up,
        g_down,
    )


def solution(mesh):
    row, act, vec = P("shard", None), P("replica", "shard", None), P("shard")
    in_specs = (act, vec, row, row, row, vec, row, row, row, act)
    out_specs = (act, act, vec, row, row, row, vec, row, row, row)
    return jax.shard_map(local, mesh=mesh, in_specs=in_specs, out_specs=out_specs, check_vma=False)
```

```python
import jax
import jax.numpy as jnp
from jax import lax
from jax.sharding import PartitionSpec as P
from jax.experimental import pallas as pl
from jax.experimental.pallas import tpu as pltpu

MESH = pl.DeviceIdType.MESH
BF = jnp.bfloat16
F32 = jnp.float32
EPS = 1e-05


def place():
    s = lax.axis_index("shard")
    r = lax.axis_index("replica")
    xl, y = s // 4, s % 4
    z, xh, c = r // 4, (r // 2) % 2, r % 2
    return xl, xh, y, z, c


def device(x, y, z, c):
    x, y, z = (x + 4) % 4, (y + 4) % 4, (z + 4) % 4
    return ((x % 2) * 4 + y, z * 4 + (x // 2) * 2 + c)


def remote(src, dst, send, recv, to):
    return pltpu.make_async_remote_copy(
        src_ref=src, dst_ref=dst, send_sem=send, recv_sem=recv, device_id=to, device_id_type=MESH
    )


def greet(devices):
    barrier = pltpu.get_barrier_semaphore()
    for to in devices:
        pl.semaphore_signal(barrier, inc=1, device_id=to, device_id_type=MESH)
    pl.semaphore_wait(barrier, len(devices))


def mul(left, right):
    return lax.dot_general(left, right, (((1,), (0,)), ((), ())), preferred_element_type=F32)


def times_rows(left, right):
    return lax.dot_general(left, right, (((1,), (1,)), ((), ())), preferred_element_type=F32)


def normalize(values):
    scale = lax.rsqrt(jnp.mean(values * values, axis=-1, keepdims=True) + EPS)
    return values * scale, scale


def norm_back(grad_normed, normed, scale):
    return scale * (grad_normed - normed * jnp.mean(grad_normed * normed, axis=-1, keepdims=True))


def loop(count, body):
    def step(i, carry):
        body(i)
        return carry

    lax.fori_loop(0, count, step, 0)


def chunk(i, size):
    return pl.ds(pl.multiple_of(i * size, size), size)


def flat(value):
    return value.reshape(-1, value.shape[-1])


ORDERS = ("XYZ", "YZX", "ZXY") * 2
SIZES = {"X": (1, 4, 1, 4), "Y": (2, 1, 2, 4), "Z": (2, 4, 2, 1)}


def dims_left(order, phase):
    sizes = [2, 4, 2, 4]
    for axis in order[: phase + 1]:
        for i in {"X": (0, 2), "Y": (1,), "Z": (3,)}[axis]:
            sizes[i] = 1
    return tuple(n for n in sizes if n > 1)


def halves(columns):
    first = columns // 256 * 128
    return (0, first), (first, columns - first)


EARLY = 2048
WIDE = 1024
LEAD = (2, 4, 2, 4, 16)


def put(at, axis, q):
    if axis == "X":
        at[0], at[2] = q % 2, q // 2
    else:
        at[1 if axis == "Y" else 3] = q


def quarter_at(axis, q):
    at = [slice(None)] * 4
    put(at, axis, q)
    return tuple(at)


def turn(source, target):
    size = 128

    def one(i):
        target[:, :, :, :, :, chunk(i, size)] = source[chunk(i, size)].T.reshape(LEAD + (size,))

    loop(source.shape[0] // size, one)


SWAPS = ("tokens", "cot", "gated0", "gated1", "mix", "act", "gam", "gmix", "fore", "back")
TILE = 256


def block_kernel(
    tokens, cot, w_in, w_out, w_gate, w_up, w_down, gains, taps_in,
    o_win, o_wd, o_resid, o_grad_resid, o_vecs,
    o_in_t, o_mid_t, o_hidden, o_gg, o_gu, o_proj, o_gated, o_mix, o_cot_t, o_small, *rest,
):
    begun, rest = [rest[7 * t : 7 * t + 7] for t in range(3)], rest[21:]
    (
        win, wout, wgu, wd, ext, tok2, cot2, act_in, proj, mixed, conv, gated, part, box_mix, box_gam,
    resid, normed, act_mid, hidden, held, gg, gu, gmix, gconv, gproj, vecs, small, scale_mid, mid_t, cot_t,
    local_sem, send_sem, recv_sem, core_send, core_recv, out_sem, early_send, early_recv,
    ) = rest
    xl, xh, y, z, c = place()
    x = xh * 2 + xl
    shard, replica = lax.axis_index("shard"), lax.axis_index("replica")
    own = xl * 4 + y
    length, width = tokens.shape
    half = width // 2
    ff = wd.shape[2]
    rows = wd.shape[1]
    mine = z % 2
    xp, xm = device(x + 1, y, z, c), device(x - 1, y, z, c)
    yp, ym = device(x, y + 1, z, c), device(x, y - 1, z, c)
    zp, zm = device(x, y, z + 1, c), device(x, y, z - 1, c)
    sibling = device(x, y, z, 1 - c)
    nxt, prv = ((shard + 1) % 8, replica), ((shard + 7) % 8, replica)
    first, last = shard == 0, shard == 7

    ext[own] = jnp.concatenate([gains[...].astype(F32), taps_in[...].astype(F32), jnp.zeros((27, 128), F32)], axis=0).astype(BF)
    copies = []
    for i in range(3):
        copies.append((w_in.at[:, pl.ds(pl.multiple_of(i * width + c * half, 128), half)], win.at[own, :, pl.ds(i * half, half)]))
    copies.append((w_gate.at[:, pl.ds(pl.multiple_of(c * ff, 128), ff)], wgu.at[0, own]))
    copies.append((w_up.at[:, pl.ds(pl.multiple_of(c * ff, 128), ff)], wgu.at[1, own]))
    copies.append((w_out, wout.at[own]))
    copies.append((w_down.at[:, pl.ds(pl.multiple_of(c * ff, 128), ff)], wd.at[own]))
    copies.append((tokens, tok2.at[pl.ds(0, length)]))
    copies.append((cot, cot2.at[pl.ds(0, length)]))
    loads = [pltpu.make_async_copy(a, b, local_sem.at[i]) for i, (a, b) in enumerate(copies)]
    for cp in loads:
        cp.start()
    greet([xp, xm, yp, ym, zp, zm, sibling, nxt, prv])

    pending, stores, used = [], [], []

    def store(src, dst):
        stores.append(pltpu.make_async_copy(src, dst, out_sem.at[len(used)]))
        used.append(dst)
        stores[-1].start()

    ending = []

    def fire(cp):
        if ending:
            cp.wait_send()
        else:
            cp.start()
            pending.append(cp.wait_send)

    owner = c == xl

    def only(condition, *bodies):
        before = len(pending)

        @pl.when(condition)
        def _():
            for body in bodies:
                body(WOUT)

        del pending[before:]

    def swap(name, src, dst, to=None):
        k = SWAPS.index(name)
        return remote(src, dst, core_send.at[k], core_recv.at[k], sibling if to is None else to)

    def wd_part(g, u):
        return wd.at[u, pl.ds(pl.multiple_of(g * (rows // 4), rows // 4), rows // 4)]

    parts = [
        (lambda g, u: ext.at[u], False),
        (lambda g, u: win.at[u], False),
        (lambda g, u: wgu.at[g, u], True),
        (lambda g, u: wout.at[u], False),
        (wd_part, True),
        (lambda g, u: wd.at[u, pl.ds(rows // 2, rows // 2)], False),
    ]
    keys, count = {}, 0
    for p in range(len(parts)):
        names = ["y+", "y-", "f+", "f-"]
        for dy in (0, -1, 1, 2):
            for h in (0, 1):
                names.append(("x", dy, h))
                if parts[p][1]:
                    names.append(("z", 1, dy, h))
                    if dy:
                        names.append(("z", 0, dy, h))
        for name in names:
            keys[p, name] = count
            count += 1
    assert count == COPIES

    def send(view, to, k):
        fire(remote(view, view, send_sem.at[k], recv_sem.at[k], to))

    def got(view, k):
        if ending:
            return
        remote(view, view, send_sem.at[k], recv_sem.at[k], yp).wait_recv()

    def cut(view, h):
        hr = view.shape[0] // 2
        return view.at[pl.ds(h * hr, hr)]

    def at_y(dy):
        return xl * 4 + (y + dy + 4) % 4

    def over(dy):
        return (1 - xl) * 4 + (y + dy + 4) % 4

    def send_x(p, dy, h):
        send(cut(parts[p][0](mine, at_y(dy)), h), (xp, xm)[h], keys[p, ("x", dy, h)])

    def send_z(p, other, dy, h):
        if parts[p][1]:
            u = over(dy) if other else at_y(dy)
            send(cut(parts[p][0](mine, u), h), (zp, zm)[h], keys[p, ("z", other, dy, h)])

    def launch_y(p):
        view = parts[p][0]
        send(view(mine, own), yp, keys[p, "y+"])
        send(view(mine, own), ym, keys[p, "y-"])

    def launch_x(p):
        for h in (0, 1):
            send_x(p, 0, h)

    def stage_a(p):
        view = parts[p][0]
        got(view(mine, at_y(-1)), keys[p, "y+"])
        send(cut(view(mine, at_y(-1)), 0), yp, keys[p, "f+"])
        for h in (0, 1):
            send_z(p, 0, -1, h)
            send_x(p, -1, h)
        got(view(mine, at_y(1)), keys[p, "y-"])
        send(cut(view(mine, at_y(1)), 1), ym, keys[p, "f-"])
        for h in (0, 1):
            send_z(p, 0, 1, h)
            send_x(p, 1, h)

    def stage_b(p):
        view = parts[p][0]
        for h in (0, 1):
            got(cut(view(mine, at_y(2)), h), keys[p, ("f+", "f-")[h]])
            send_z(p, 0, 2, h)
            send_x(p, 2, h)

    def stage_c(p, *dys):
        view = parts[p][0]
        for dy in dys or (0, -1, 1, 2):
            for h in (0, 1):
                got(cut(view(mine, over(dy)), h), keys[p, ("x", dy, h)])
                send_z(p, 1, dy, h)

    def stage_d(p):
        view = parts[p][0]
        for h in (0, 1):
            for dy in (0, -1, 1, 2):
                if dy:
                    got(cut(view(1 - mine, at_y(dy)), h), keys[p, ("z", 0, dy, h)])
                got(cut(view(1 - mine, over(dy)), h), keys[p, ("z", 1, dy, h)])

    EXT, WIN, WGU, WOUT, WDZ, WDX = range(6)
    lower, upper = pl.ds(0, length), pl.ds(length, length)
    launch_y(EXT)
    launch_x(EXT)
    for cp in loads[3:5]:
        cp.wait()
    launch_y(WGU)
    launch_x(WGU)
    for cp in loads[:3]:
        cp.wait()
    launch_y(WIN)
    launch_x(WIN)
    for cp in loads[7:]:
        cp.wait()
    fire(swap("tokens", tok2.at[lower], tok2.at[upper]))
    fire(swap("cot", cot2.at[lower], cot2.at[upper]))
    for cp in loads[5:7]:
        cp.wait()
    only(owner, launch_x)
    launch_x(WDZ)
    launch_x(WDX)
    for stage in (stage_a, stage_b, stage_c):
        stage(EXT)
    for u in range(8):
        vecs[:, pl.ds(u * 128, 128)] = ext[u, pl.ds(0, 16)].astype(F32)
    small[...] = jnp.zeros_like(small)
    mixed[:, pl.ds(0, 8)] = jnp.zeros((2, 8, half), F32)
    gconv[:, pl.ds(length, 8)] = jnp.zeros((2, 8, half), F32)
    swap("tokens", tok2.at[lower], tok2.at[upper]).wait_recv()
    rc = 32

    def norm_in_step(i):
        v, _ = normalize(tok2[chunk(i, rc)].astype(F32))
        act_in[chunk(i, rc)] = (v * vecs[0:1]).astype(BF)

    loop(2 * length // rc, norm_in_step)
    turn(act_in, mid_t)
    store(mid_t, o_in_t)
    in_store = stores.pop()
    stage_c(WGU, 0)
    stage_a(WGU)
    only(owner, launch_y)
    stage_a(WIN)
    launch_y(WDZ)
    stage_c(WGU, -1, 1)
    stage_b(WGU)
    only(owner, stage_a)
    launch_y(WDX)
    stage_b(WIN)
    stage_c(WGU, 2)
    stage_a(WDZ)
    swap("cot", cot2.at[lower], cot2.at[upper]).wait_recv()
    turn(cot2, cot_t)
    store(cot_t, o_cot_t)
    stage_c(WIN)

    def proj_step(j):
        proj[:, chunk(j, TILE)] = mul(act_in[...], flat(win[:, :, chunk(j, TILE)]))

    store(win, o_win)
    store(vecs, o_vecs)
    loop(3 * half // TILE, proj_step)

    def b_of(at):
        return proj[at, pl.ds(0, half)]

    def c_of(at):
        return proj[at, pl.ds(half, half)]

    def x_of(at):
        return proj[at, pl.ds(2 * half, half)]

    def mixed_step(i):
        for q in (0, 1):
            at = pl.ds(pl.multiple_of(q * length + i * rc, rc), rc)
            mixed[q, pl.ds(pl.multiple_of(8 + i * rc, 8), rc)] = (b_of(at) * x_of(at)).astype(BF).astype(F32)

    loop(length // rc, mixed_step)
    fore = swap("fore", mixed.at[:, pl.ds(length, 8)], mixed.at[:, pl.ds(0, 8)], nxt)
    back = swap("back", gconv.at[:, pl.ds(0, 8)], gconv.at[:, pl.ds(length, 8)], prv)

    @pl.when(jnp.logical_not(last))
    def _():
        fore.start()

    only(owner, stage_b)
    stage_c(WDZ, 0)
    stage_a(WDX)

    @pl.when(jnp.logical_not(first))
    def _():
        fore.wait_recv()

    taps = [vecs[pl.ds(2 + k, 1), pl.ds(pl.multiple_of(c * half, 128), half)] for k in range(3)]
    rq = 64

    def conv_step(i):
        for q in (0, 1):
            window = mixed[q, pl.ds(pl.multiple_of(i * rq, 8), rq + 8)]
            value = taps[0] * window[6 : 6 + rq] + taps[1] * window[7 : 7 + rq] + taps[2] * window[8 : 8 + rq]
            at = pl.ds(pl.multiple_of(q * length + i * rq, rq), rq)
            conv[at] = value
            gated[at, pl.ds(pl.multiple_of(c * half, 128), half)] = (c_of(at) * value).astype(BF)

    loop(length // rq, conv_step)
    gated_mine = gated.at[:, pl.ds(pl.multiple_of(c * half, 128), half)]
    gated_other = gated.at[:, pl.ds(pl.multiple_of((1 - c) * half, 128), half)]
    fire(swap("gated0", gated_mine.at[lower], gated_mine.at[upper]))
    fire(swap("gated1", gated_mine.at[upper], gated_mine.at[lower]))
    stage_b(WDZ)
    stage_c(WDZ, -1, 1)
    only(jnp.logical_not(owner), stage_c)
    wout_mine = wout.at[pl.ds(pl.multiple_of(c * 4, 4), 4)]

    def mix_step(j):
        part[:, chunk(j, TILE)] = mul(gated_mine[...], flat(wout_mine[:, :, chunk(j, TILE)]))

    loop(width // TILE, mix_step)
    mix_swap = swap("mix", part.at[upper], box_mix)
    mix_swap.start()
    stage_b(WDX)
    mix_swap.wait_recv()

    def norm_mid_step(i):
        at = chunk(i, rc)
        v = tok2[at].astype(F32) + part[at] + box_mix[at]
        n, s = normalize(v)
        resid[at] = v
        normed[at] = n
        scale_mid[at] = jnp.broadcast_to(s, (rc, 128))
        act_mid[at] = (n * vecs[1:2]).astype(BF)

    loop(length // rc, norm_mid_step)
    store(resid, o_resid)
    act_swap = swap("act", act_mid.at[lower], act_mid.at[upper])
    act_swap.start()
    stage_c(WDZ, 2)
    act_swap.wait_recv()
    in_store.wait()
    turn(act_mid, mid_t)
    store(mid_t, o_mid_t)
    stage_d(WGU)

    where = {"X": x, "Y": y, "Z": z}
    near = {"X": (xm, xp), "Y": (ym, yp), "Z": (zm, zp)}
    eh = EARLY // 2

    def early_at(t, step):
        axis = ORDERS[t][0]
        return quarter_at(axis, (where[axis] + step) % 4)

    def early_fill(t, step):
        at = early_at(t, step)
        lead = dims_left(ORDERS[t], 0) + (16, WIDE)
        tall, right = flat((mid_t, mid_t, cot_t)[t][at]), (gg, gu, hidden)[t]

        def one(j):
            value = mul(tall, right[:, chunk(j, WIDE)]).astype(BF)
            held[(t,) + at + (slice(None), chunk(j, WIDE))] = value.reshape(lead)

        loop(EARLY // WIDE, one)

    def early_cols(view, h):
        return view.at[(slice(None),) * (len(view.shape) - 1) + (pl.ds(h * eh, eh),)]

    def keep(t):
        store(held.at[(t,) + early_at(t, 0)], begun[t][0])
        store(early_cols(held.at[(t,) + early_at(t, 1)], 0), begun[t][1])
        store(early_cols(held.at[(t,) + early_at(t, 3)], 1), begun[t][2])

    def early_copy(t, k):
        to_right = k in (0, 2)
        h = (0, 1, 1, 0)[k]
        step = 2 if k < 2 else (1 if to_right else 3)
        src = early_cols(held.at[(t,) + early_at(t, step)], h)
        dst = begun[t][3 + k]
        to = near[ORDERS[t][0]][1 if to_right else 0]
        return remote(src, dst, early_send.at[t * 4 + k], early_recv.at[t * 4 + k], to)

    def gate_step(j):
        at = chunk(j, TILE)
        gate = mul(act_mid[...], flat(wgu[0, :, :, at]))
        up = mul(act_mid[...], flat(wgu[1, :, :, at]))
        sig = jax.nn.sigmoid(gate)
        silu = gate * sig
        hidden[:, at] = (silu * up).astype(BF)
        factor = up * (sig * (1.0 + gate * (1.0 - sig)))
        spot = (slice(None),) * 4 + (chunk(j % (EARLY // TILE), TILE),)
        held[(j // (EARLY // TILE), 0) + spot] = factor.astype(BF).reshape(LEAD[1:] + (TILE,))
        held[(j // (EARLY // TILE), 1) + spot] = silu.astype(BF).reshape(LEAD[1:] + (TILE,))

    loop(ff // TILE, gate_step)
    store(hidden, o_hidden)
    early_fill(2, 2)
    fire(early_copy(2, 0))
    fire(early_copy(2, 1))
    early_fill(2, 1)
    fire(early_copy(2, 2))
    stage_c(WDX)
    stage_d(WDZ)

    def grad_hidden_step(j):
        at = chunk(j, TILE)
        g = mul(cot2[...], flat(wd[:, :, at]))
        spot = (slice(None),) * 4 + (chunk(j % (EARLY // TILE), TILE),)
        gg[:, at] = (g * flat(held[(j // (EARLY // TILE), 0) + spot]).astype(F32)).astype(BF)
        gu[:, at] = (g * flat(held[(j // (EARLY // TILE), 1) + spot]).astype(F32)).astype(BF)

    loop(ff // TILE, grad_hidden_step)
    store(gg.at[:, pl.ds(EARLY, ff - EARLY)], o_gg)
    store(gu.at[:, pl.ds(EARLY, ff - EARLY)], o_gu)
    store(wd, o_wd)
    for t in (0, 1):
        early_fill(t, 2)
        fire(early_copy(t, 0))
        fire(early_copy(t, 1))
    for t in (0, 1):
        early_fill(t, 1)
        fire(early_copy(t, 2))
    early_fill(2, 3)
    fire(early_copy(2, 3))
    swap("mix", part.at[upper], box_mix).wait_send()

    def gam_step(j):
        u = pl.ds(j * 2, 2)
        part[:, chunk(j, TILE)] = times_rows(gg[...], flat(wgu[0, u])) + times_rows(gu[...], flat(wgu[1, u]))

    loop(4, gam_step)
    gam_swap = swap("gam", part.at[upper], box_gam)
    gam_swap.start()
    for t in (0, 1):
        early_fill(t, 3)
        fire(early_copy(t, 3))
    gam_swap.wait_recv()

    def resid_step(i):
        at = chunk(i, rc)
        g = part[at] + box_gam[at]
        n = normed[at]
        small[1:2] = small[1:2] + jnp.sum(g * n, axis=0, keepdims=True)
        full = cot2[at].astype(F32) + norm_back(g * vecs[1:2], n, scale_mid[at, 0:1])
        box_gam[at] = full
        gmix[at] = full.astype(BF)

    loop(length // rc, resid_step)
    gmix_swap = swap("gmix", gmix.at[lower], gmix.at[upper])
    gmix_swap.start()
    for t in (0, 1, 2):
        early_fill(t, 0)
        keep(t)
    gam_swap.wait_send()

    def ffn_step(j):
        u = pl.ds(j * 2, 2)
        part[:, chunk(j, TILE)] = times_rows(hidden[...], flat(wd[u]))

    loop(4, ffn_step)
    store(box_gam, o_grad_resid)
    gmix_swap.wait_recv()
    for q in (0, 1):
        box_mix[:, pl.ds(q * half, half)] = times_rows(gmix[pl.ds(q * length, length)], flat(wout_mine[...]))

    def gconv_step(i):
        for q in (0, 1):
            at = pl.ds(pl.multiple_of(q * length + i * rc, rc), rc)
            window = mixed[q, pl.ds(pl.multiple_of(i * rc, 8), rc + 8)]
            g = box_mix[pl.ds(pl.multiple_of(i * rc, rc), rc), pl.ds(q * half, half)]
            gc = g * c_of(at)
            gconv[q, pl.ds(pl.multiple_of(i * rc, 8), rc)] = gc
            gproj[at, pl.ds(half, half)] = (g * conv[at]).astype(BF)
            for k in range(3):
                spot = (pl.ds(2 + k, 1), pl.ds(pl.multiple_of(c * half, 128), half))
                small[spot] = small[spot] + jnp.sum(gc * window[6 + k : 6 + k + rc], axis=0, keepdims=True)

    loop(length // rc, gconv_step)

    @pl.when(jnp.logical_not(first))
    def _():
        back.start()

    @pl.when(jnp.logical_not(last))
    def _():
        back.wait_recv()

    def gproj_step(i):
        for q in (0, 1):
            at = pl.ds(pl.multiple_of(q * length + i * rc, rc), rc)
            window = gconv[q, pl.ds(pl.multiple_of(i * rc, 8), rc + 8)]
            gm = taps[2] * window[0:rc] + taps[1] * window[1 : rc + 1] + taps[0] * window[2 : rc + 2]
            gproj[at, pl.ds(0, half)] = (gm * x_of(at)).astype(BF)
            gproj[at, pl.ds(2 * half, half)] = (gm * b_of(at)).astype(BF)

    loop(length // rc, gproj_step)
    swap("gated0", gated_other.at[upper], gated_other.at[upper]).wait_recv()
    swap("gated1", gated_other.at[lower], gated_other.at[lower]).wait_recv()
    store(gproj, o_proj)
    store(gated, o_gated)
    store(gmix, o_mix)
    store(small, o_small)
    for t in range(3):
        for k in range(4):
            early_copy(t, k).wait_recv()
    for wait in pending:
        wait()

    ending.append(True)
    only(owner, launch_x, launch_y, stage_a, stage_b)
    act_swap.wait_send()
    gmix_swap.wait_send()

    @pl.when(jnp.logical_not(last))
    def _():
        fore.wait_send()

    @pl.when(jnp.logical_not(first))
    def _():
        back.wait_send()

    for cp in stores:
        cp.wait()


COPIES = 6 * 12 + 2 * 14


def block_call(tokens, cot, w_in, w_out, w_gate, w_up, w_down, gains, taps):
    length, width = tokens.shape
    rows, ff = w_in.shape[0], w_gate.shape[1] // 2
    half = width // 2
    two = 2 * length
    hbm = pl.BlockSpec(memory_space=pltpu.HBM)
    vm = pl.BlockSpec(memory_space=pltpu.VMEM)

    def out(*shape, dtype=BF):
        return jax.ShapeDtypeStruct(shape, dtype)

    def mem(*shape, dtype=BF):
        return pltpu.VMEM(shape, dtype)

    firsts = [dims_left(ORDERS[t], 0) + (16,) for t in range(3)]
    early = [out(*firsts[t], EARLY if k == 0 else EARLY // 2) for t in range(3) for k in range(7)]
    dma = pltpu.SemaphoreType.DMA
    return pl.pallas_call(
        block_kernel,
        out_shape=(
            out(8, rows, 3 * half), out(8, rows, ff), out(length, width, dtype=F32), out(length, width, dtype=F32),
            out(16, width, dtype=F32), out(*LEAD, two), out(*LEAD, two), out(two, ff),
            out(two, ff - EARLY), out(two, ff - EARLY), out(two, 3 * half), out(two, width), out(two, width), out(*LEAD, two),
            out(8, width, dtype=F32), *early,
        ),
        in_specs=[hbm] * 7 + [vm] * 2,
        out_specs=(hbm,) * 36,
        scratch_shapes=[
            mem(8, rows, 3 * half), mem(8, rows, width), mem(2, 8, rows, ff), mem(8, rows, ff), mem(8, 32, 128),
            mem(two, width), mem(two, width), mem(two, width), mem(two, 3 * half, dtype=F32),
            mem(2, length + 8, half, dtype=F32), mem(two, half, dtype=F32), mem(two, width), mem(two, width, dtype=F32),
            mem(length, width, dtype=F32), mem(length, width, dtype=F32), mem(length, width, dtype=F32),
            mem(length, width, dtype=F32), mem(two, width),
            mem(two, ff), mem(3, *LEAD, EARLY), mem(two, ff), mem(two, ff), mem(two, width),
            mem(2, length + 8, half, dtype=F32), mem(two, 3 * half), mem(16, width, dtype=F32), mem(8, width, dtype=F32),
            mem(length, 128, dtype=F32), mem(*LEAD, two), mem(*LEAD, two),
            dma((9,)), dma((COPIES,)), dma((COPIES,)), dma((len(SWAPS),)), dma((len(SWAPS),)), dma((48,)), dma((12,)), dma((12,)),
        ],
        compiler_params=pltpu.CompilerParams(collective_id=1, has_side_effects=True, vmem_limit_bytes=62 << 20),
    )(tokens, cot, w_in, w_out, w_gate, w_up, w_down, gains, taps)
COUNT = 6
INS = 16


def reduce_kernel(*refs):
    n = COUNT
    ins, refs = refs[:INS], refs[INS:]
    begun, refs = refs[:21], refs[21:]
    outs, refs = refs[:8], refs[8:]
    held, refs = refs[:n], refs[n:]
    relay, refs = [refs[6 * t : 6 * t + 6] for t in range(n)], refs[6 * n :]
    takes, refs = [refs[6 * t : 6 * t + 6] for t in range(n)], refs[6 * n :]
    bufs, refs = refs[:INS], refs[INS:]
    turned, refs = refs[:1], refs[1:]
    (sums, box_ffn, box_gai, out_res), refs = refs[:4], refs[4:]
    local_sem, send_sem, recv_sem, spread_send, spread_recv, core_send, core_recv = refs
    o_gate, o_up, o_down, o_in, o_out, o_small, result, grad_tokens = outs
    xl, xh, y, z, c = place()
    x = xh * 2 + xl
    loads = [pltpu.make_async_copy(a, b, local_sem.at[i]) for i, (a, b) in enumerate(zip(ins, bufs))]
    in_t, gproj, cot_t, hidden, gated, gmix, mid_t, gu, win, grad_resid, vecs, tokens, small, gg, wd, resid = bufs
    (gated_t,) = turned
    half = gproj.shape[1] // 3
    ff = hidden.shape[1]
    length = tokens.shape[0]
    width = half * 2
    quarter = half // 2
    where = {"X": x, "Y": y, "Z": z}
    near = {
        "X": (device(x - 1, y, z, c), device(x + 1, y, z, c)),
        "Y": (device(x, y - 1, z, c), device(x, y + 1, z, c)),
        "Z": (device(x, y, z - 1, c), device(x, y, z + 1, c)),
    }
    taken = []
    for t in range(3):
        axis = ORDERS[t][0]
        p, low, high = where[axis], pl.ds(0, EARLY // 2), pl.ds(EARLY // 2, EARLY // 2)
        lead = (slice(None),) * len(dims_left(axis, 0)) + (slice(None),)
        boxes = (
            held[t].at[quarter_at(axis, p)],
            held[t].at[quarter_at(axis, (p + 1) % 4)].at[lead + (low,)],
            held[t].at[quarter_at(axis, (p + 3) % 4)].at[lead + (high,)],
            relay[t][0],
            relay[t][1],
            takes[t][0].at[lead + (high,)],
            takes[t][1].at[lead + (low,)],
        )
        for k in (1, 2, 3, 4, 0, 5, 6):
            i = 7 * t + k
            taken.append(pltpu.make_async_copy(begun[i], boxes[k], local_sem.at[INS + i]))
    firsts = [cp for t in range(3) for cp in taken[7 * t : 7 * t + 4]]
    others = [cp for t in range(3) for cp in taken[7 * t + 4 : 7 * t + 7]]
    for cp in (*firsts, *loads[:8], *others, *loads[8:]):
        cp.start()
    across, beyond = device(x + 2, y, z, c), device(x, y, z + 2, c)
    sibling = device(x, y, z, 1 - c)
    greet([*near["X"], *near["Y"], *near["Z"], across, beyond, sibling])
    pending = []

    def index(order, phase, q):
        at = [slice(None)] * 4
        for a in order[:phase]:
            put(at, a, where[a])
        put(at, order[phase], q)
        return tuple(at)

    def key(t, phase, k):
        return (t * 3 + phase) * 6 + k

    def ship(src, dst, to, t, phase, k):
        cp = remote(src, dst, send_sem.at[key(t, phase, k)], recv_sem.at[key(t, phase, k)], to)
        cp.start()
        pending.append(cp)

    def arrived(dst, t, phase, k):
        remote(dst, dst, send_sem.at[key(t, phase, k)], recv_sem.at[key(t, phase, k)], sibling).wait_recv()

    def cols(view, h, t):
        at, size = halves(held[t].shape[-1])[h]
        lead = len(view.shape) - 1
        return view.at[(slice(None),) * lead + (pl.ds(at, size),)]

    def part(ref, t, phase, q, h):
        return cols(ref.at[index(ORDERS[t], phase, q)], h, t)

    def buffers(t, phase):
        ra, rb = relay[t][2 * phase : 2 * phase + 2]
        tl, tr = takes[t][2 * phase : 2 * phase + 2]
        return ra, rb, tl, tr

    def each(dims, body):
        total = 1
        for d in dims:
            total *= d

        def step(i, carry):
            at, rest = [], i
            for d in reversed(dims):
                at.append(rest % d)
                rest = rest // d
            body(tuple(reversed(at)))
            return carry

        if total == 1:
            body(())
        else:
            lax.fori_loop(0, total, step, 0)

    def full(order, phase, q, at):
        idx, k = list(index(order, phase, q)), 0
        for i in range(4):
            if isinstance(idx[i], slice):
                idx[i] = at[k]
                k += 1
        return tuple(idx)

    def begin(t, phase, first=True, second=True):
        order = ORDERS[t]
        p = where[order[phase]]
        left, right = near[order[phase]]
        ra, rb, tl, tr = buffers(t, phase)
        src = held[t]
        far_q, next_q, last_q = (p + 2) % 4, (p + 1) % 4, (p + 3) % 4
        if first:
            ship(part(src, t, phase, far_q, 0), ra, right, t, phase, 0)
            ship(part(src, t, phase, far_q, 1), rb, left, t, phase, 1)
        if second:
            ship(part(src, t, phase, next_q, 1), cols(tl, 1, t), right, t, phase, 2)
            ship(part(src, t, phase, last_q, 0), cols(tr, 0, t), left, t, phase, 3)

    def middle(t, phase):
        order = ORDERS[t]
        p = where[order[phase]]
        left, right = near[order[phase]]
        ra, rb, tl, tr = buffers(t, phase)
        dims = dims_left(order, phase)
        begun_here = t < 3 and phase == 0
        if begun_here:
            for cp in taken[7 * t : 7 * t + 4]:
                cp.wait()
        for h, (box, q, to, dst) in enumerate(((ra, (p + 1) % 4, right, tl), (rb, (p + 3) % 4, left, tr))):
            if not begun_here:
                arrived(box, t, phase, h)
            at0, size = halves(held[t].shape[-1])[h]

            def add(at, box=box, q=q, at0=at0, size=size):
                slab = full(order, phase, q, at) + (slice(None), pl.ds(at0, size))
                held[t][slab] = (held[t][slab].astype(F32) + box[at].astype(F32)).astype(BF)

            each(dims, add)
            ship(part(held[t], t, phase, q, h), cols(dst, h, t), to, t, phase, 4 + h)

    def finish(t, phase):
        order = ORDERS[t]
        p = where[order[phase]]
        ra, rb, tl, tr = buffers(t, phase)
        dims = dims_left(order, phase)
        if t < 3 and phase == 0:
            for cp in taken[7 * t + 4 : 7 * t + 7]:
                cp.wait()
        else:
            arrived(cols(tl, 1, t), t, phase, 2)
            arrived(cols(tr, 0, t), t, phase, 3)
        arrived(cols(tl, 0, t), t, phase, 4)
        arrived(cols(tr, 1, t), t, phase, 5)

        def add(at):
            slab = full(order, phase, p, at)
            held[t][slab] = (held[t][slab].astype(F32) + tl[at].astype(F32) + tr[at].astype(F32)).astype(BF)

        each(dims, add)

    def fill(t, step):
        axis = ORDERS[t][0]
        at = [slice(None)] * 4
        put(at, axis, (where[axis] + step) % 4)
        at = tuple(at)
        lead = dims_left(ORDERS[t], 0)

        def block(left, right, start, cols_n, put_at):
            rows = flat(left[at])

            value = mul(rows, right[:, pl.ds(pl.multiple_of(start, 128), cols_n)]).astype(BF)
            held[t][at + (slice(None), pl.ds(put_at, cols_n))] = value.reshape(lead + (16, cols_n))

        i = t % 3
        left, right = (mid_t, mid_t, cot_t)[i], (gg, gu, hidden)[i]
        block(left, right, EARLY if i == 2 else 0, ff - EARLY, 0)
        block(in_t, gproj, i * half, half, ff - EARLY)
        if i:
            block(gated_t, gmix, c * half + (i - 1) * quarter, quarter, ff - EARLY + half)

    def swap(k, dst):
        return remote(sums.at[pl.ds(length, length)], dst, core_send.at[12 + k], core_recv.at[12 + k], sibling)

    def gai_step(j):
        sums[:, chunk(j, TILE)] = times_rows(gproj[...], flat(win[pl.ds(j * 2, 2)]))

    def ffn_step(j):
        sums[:, chunk(j, TILE)] = times_rows(hidden[...], flat(wd[pl.ds(j * 2, 2)]))

    def final_step(i):
        at = chunk(i, 32)
        g = sums[at] + box_gai[at]
        normed, scale = normalize(tokens[at].astype(F32))
        small[0:1] = small[0:1] + jnp.sum(g * normed, axis=0, keepdims=True)
        grad_resid[at] = grad_resid[at] + norm_back(g * vecs[0:1], normed, scale)

    def own_ffn_step(i):
        at = chunk(i, 32)
        resid[at] = resid[at] + sums[at]

    def result_step(i):
        at = chunk(i, 32)
        out_res[at] = (resid[at] + box_ffn[at]).astype(BF)

    for t in (0, 1, 2):
        middle(t, 0)
    for cp in loads[:6]:
        cp.wait()
    turn(gated, gated_t)
    fill(5, 2)
    begin(5, 0, second=False)
    for cp in loads[6:9]:
        cp.wait()
    loop(4, gai_step)
    gai_swap = swap(0, box_gai)
    gai_swap.start()
    fill(4, 2)
    begin(4, 0, second=False)
    for t in (5, 4):
        fill(t, 1)
        fill(t, 3)
        begin(t, 0, first=False)
    for cp in loads[9:]:
        cp.wait()
    gai_swap.wait_recv()
    loop(length // 32, final_step)
    back = [pltpu.make_async_copy(grad_resid, grad_tokens, local_sem.at[INS + 21])]
    back[0].start()
    tall = jnp.concatenate([small[...], jnp.zeros((120, width), F32)], axis=0)
    held[3][:, :, :, :, :, pl.ds(ff - EARLY + half, 128)] = tall.T.astype(BF).reshape(2, 4, 2, 4, 16, 128)
    fill(3, 2)
    begin(3, 0, second=False)
    fill(3, 1)
    fill(3, 3)
    begin(3, 0, first=False)
    middle(5, 0)
    middle(4, 0)
    for t in (0, 1, 2):
        finish(t, 0)
        begin(t, 1)
    middle(3, 0)
    for t in (5, 4, 3):
        fill(t, 0)
    for t in (0, 1, 2):
        middle(t, 1)
    gai_swap.wait_send()
    loop(4, ffn_step)
    ffn_swap = swap(1, box_ffn)
    ffn_swap.start()
    loop(length // 32, own_ffn_step)
    for t in (5, 4, 3):
        finish(t, 0)
        begin(t, 1)
    for t in (0, 1, 2):
        finish(t, 1)
        begin(t, 2)
    ffn_swap.wait_recv()
    loop(length // 32, result_step)
    back.append(pltpu.make_async_copy(out_res, result, local_sem.at[INS + 22]))
    back[1].start()
    for t in (3, 4, 5):
        middle(t, 1)
    for t in (0, 1, 2):
        middle(t, 2)
    for t in (3, 4, 5):
        finish(t, 1)
        begin(t, 2)
    for t in (0, 1, 2):
        finish(t, 2)
    late = ff - EARLY
    pieces = []
    for t in range(n):
        wide = (o_gate, o_up, o_down)[t % 3]
        if t < 3:
            pieces.append([(0, EARLY, wide, 0, ff)])
        else:
            i = t - 3
            pieces.append([(0, late, wide, EARLY, ff), (late, half, o_in, i * width, half)])
            if i:
                pieces[-1].append((late + half, quarter, o_out, (i - 1) * quarter, half))
            else:
                pieces[-1].append((late + half, 128, o_small, 0, 128))
    base = [sum(len(p) for p in pieces[:t]) for t in range(n)]

    def spot(out, row, count, col, size):
        return out.at[pl.ds(pl.multiple_of(row, 16), count), pl.ds(pl.multiple_of(col, 128), size)]

    def landing(t, k, dx, dz):
        at, size, out, col, stride = pieces[t][k]
        slot = (xh + dx) % 2 * 4 + (z + dz + 4) % 4
        return spot(out, slot * 16, 16, col + c * stride, size)

    def pass_on(t, k, i, src, dst, to):
        key_ = (base[t] + k) * 7 + i
        cp = remote(src, dst, spread_send.at[key_], spread_recv.at[key_], to)
        cp.start()
        pending.append(cp)

    def landed(t, k, i, dx, dz):
        key_ = (base[t] + k) * 7 + i
        dst = landing(t, k, dx, dz)
        remote(dst, dst, spread_send.at[key_], spread_recv.at[key_], sibling).wait_recv()

    zm, zp = near["Z"]
    keeps = {}

    def spread(t):
        for k, (at, size, out, col, stride) in enumerate(pieces[t]):
            piece = held[t].at[xl, y, xh, z, :, pl.ds(at, size)]
            dst = landing(t, k, 0, 0)
            for i, to in enumerate((across, beyond, zp, zm)):
                pass_on(t, k, i, piece, dst, to)
            keeps[t, k] = pltpu.make_async_copy(piece, dst, local_sem.at[base[t] + k])
            keeps[t, k].start()

    def spread_more(t):
        for k in range(len(pieces[t])):
            landed(t, k, 0, 1, 0)
            mine = landing(t, k, 1, 0)
            pass_on(t, k, 4, mine, mine, zp)
            pass_on(t, k, 5, mine, mine, zm)
            landed(t, k, 1, 0, 2)
            mine = landing(t, k, 0, 2)
            pass_on(t, k, 6, mine, mine, across)

    def share(t):
        for k, (at, size, out, col, stride) in enumerate(pieces[t]):
            keeps[t, k].wait()
            landed(t, k, 2, 0, -1)
            landed(t, k, 3, 0, 1)
            landed(t, k, 4, 1, -1)
            landed(t, k, 5, 1, 1)
            landed(t, k, 6, 1, 2)
            whole = spot(out, 0, 128, col + c * stride, size)
            cp = remote(whole, whole, core_send.at[base[t] + k], core_recv.at[base[t] + k], sibling)
            cp.start()
            pending.append(cp)

    for t in (0, 1, 2):
        spread(t)
    for t in (3, 4, 5):
        middle(t, 2)
    for t in (3, 4, 5):
        finish(t, 2)
        spread(t)
    for step in (spread_more, share):
        for t in range(n):
            step(t)
    for t in range(n):
        for k, (at, size, out, col, stride) in enumerate(pieces[t]):
            dst = spot(out, 0, 128, col + (1 - c) * stride, size)
            remote(dst, dst, core_send.at[base[t] + k], core_recv.at[base[t] + k], sibling).wait_recv()
    for cp in back:
        cp.wait()
    ffn_swap.wait_send()
    for cp in pending:
        cp.wait_send()


def reduce_grads(tokens, win, wd, resid, grad_resid, vecs, in_t, mid_t, hidden, gg, gu, gproj, gated, gmix, cot_t, small, *begun):
    n = COUNT
    ins = (in_t, gproj, cot_t, hidden, gated, gmix, mid_t, gu, win, grad_resid, vecs, tokens, small, gg, wd, resid)
    width, ff, two = gated.shape[1], hidden.shape[1], gated.shape[0]
    length = two // 2
    half = width // 2
    late = ff - EARLY + half
    widths = (EARLY,) * 3 + (late + 128, late + half // 2, late + half // 2)
    lead = (2, 4, 2, 4, 16)
    held = [pltpu.VMEM(lead + (w,), BF) for w in widths]
    relay, takes = [], []
    for t in range(n):
        for phase in range(3):
            dims = dims_left(ORDERS[t], phase)
            for h in (0, 1):
                relay.append(pltpu.VMEM(dims + (16, halves(widths[t])[h][1]), BF))
                takes.append(pltpu.VMEM(dims + (16, widths[t]), BF))
    bufs = [pltpu.VMEM(a.shape, a.dtype) for a in ins]
    turned = [pltpu.VMEM(lead + (two,), BF)]
    one = pltpu.VMEM((length, width), F32)
    own = [pltpu.VMEM((two, width), F32), one, one, pltpu.VMEM((length, width), BF)]
    dma = pltpu.SemaphoreType.DMA
    hbm = pl.BlockSpec(memory_space=pltpu.HBM)
    rows = 128
    outs = (2 * ff, 2 * ff, 2 * ff, 3 * width, width, 256)
    return pl.pallas_call(
        reduce_kernel,
        out_shape=tuple(jax.ShapeDtypeStruct((rows, w), BF) for w in outs)
        + (jax.ShapeDtypeStruct((length, width), BF), jax.ShapeDtypeStruct((length, width), F32)),
        in_specs=[hbm] * len(ins + begun),
        out_specs=(hbm,) * 8,
        scratch_shapes=held + relay + takes + bufs + turned + own
        + [dma((39,)), dma((108,)), dma((108,)), dma((84,)), dma((84,)), dma((14,)), dma((14,))],
        compiler_params=pltpu.CompilerParams(collective_id=2, has_side_effects=True, vmem_limit_bytes=62 << 20),
    )(*ins, *begun)


def local(tokens, norm_in, w_in, conv_w, w_out, norm_mid, w_gate, w_up, w_down, cotangent):
    gains = jnp.stack([norm_in, norm_mid])
    kept = block_call(tokens[0], cotangent[0], w_in, w_out, w_gate, w_up, w_down, gains, conv_w.T)
    *sums, result, grad_tokens = reduce_grads(tokens[0], *kept)
    g_gate, g_up, g_down, g_in, g_out, g_small = (s.astype(F32) for s in sums)
    g_small = g_small[:, :128] + g_small[:, 128:]
    return (
        result[None],
        grad_tokens[None],
        g_small[:, 0],
        g_in,
        g_small[:, 2:5],
        g_out,
        g_small[:, 1],
        g_gate,
        g_up,
        g_down,
    )


def solution(mesh):
    row, act, vec = P("shard", None), P("replica", "shard", None), P("shard")
    in_specs = (act, vec, row, row, row, vec, row, row, row, act)
    out_specs = (act, act, vec, row, row, row, vec, row, row, row)
    return jax.shard_map(local, mesh=mesh, in_specs=in_specs, out_specs=out_specs, check_vma=False)
```
